32 devices in a mesh: groups: 2 (over x), lon: 16 (over z, y, core).
Axes of the slice: x: 2, y: 2, z: 4, core: 2. Of those that a mesh axis runs over, the one named last changes fastest.
Arguments:
- latlon_fields: bfloat16 [32, 32, 2048], P('groups', 'lon'), parts along dimension 0, may hold values from -6 to 6
- remap_table: int32 [2, 32, 2048], P(None, None, 'lon'), may hold values from 0 to 2047, as said below
- kernel_first: bfloat16 [3, 3, 64, 16], replicated, may hold values from -0.5 to 0.5
- kernel_second: bfloat16 [3, 3, 64, 64], replicated, may hold values from -0.25 to 0.25
- kernel_down: bfloat16 [3, 3, 128, 64], replicated, may hold values from -0.25 to 0.25
- kernel_coarse: bfloat16 [3, 3, 128, 128], replicated, may hold values from -0.1875 to 0.1875
- kernel_up: bfloat16 [3, 3, 64, 128], replicated, may hold values from -0.375 to 0.375
- kernel_merge: bfloat16 [3, 3, 64, 128], replicated, may hold values from -0.1875 to 0.1875
- projection: bfloat16 [8, 64], replicated, may hold values from -0.75 to 0.75
Outputs:
- forecast: float32 [16, 32, 2048], P('groups', None, 'lon'), parts along dimension 0
The draws below stay inside these ranges and needn't reach their ends.
There are 2 independent parts, one for each index of `groups`. The reference program is written for one: setup_inputs(seed, part) draws one part's arguments, and reference() takes and returns one part's arrays. A program takes and returns all parts, laid end to end along the dimension named above; an argument that names none is the same for every part. Nothing has to cross between parts.
Inputs may be any that keep to these rules, and one draw needn't show every extreme that they name: remap_table[0] is a lat-lon row below 32; remap_table[1] is a lat-lon column, and for a grid cell in column w it lies in the same block of 128 columns as w, that is between (w // 128) * 128 and (w // 128) * 128 + 127.
All inputs are finite; a program needn't handle non-finite values.
Results may differ from the reference program's by a relative error of at most 0.00084.
Values may be sent and summed in bfloat16 or wider, within the bound.
A program may use at most 128 MiB of HBM per device.

```python
import jax
import jax.numpy as jnp
from jax import lax

C = 64
C2 = 128
CIN = 16
COUT = 8
H = 32
WD = 128
W = 2048
NLAT = 32


def draw_remap_table(key, part):
    key_rows, key_cols = jax.random.split(jax.random.fold_in(key, 7))
    row_index = jnp.broadcast_to(jnp.arange(H, dtype=jnp.int32)[:, None], (H, W))
    col_index = jnp.broadcast_to(jnp.arange(W, dtype=jnp.int32)[None, :], (H, W))
    jitter_rows = jax.random.randint(key_rows, (H, W), -2, 3, dtype=jnp.int32)
    latitude = jnp.clip(row_index * NLAT // H + jitter_rows, 0, NLAT - 1)
    owners = col_index // WD
    offset = col_index % WD
    jitter_cols = jax.random.randint(key_cols, (H, W), -1, 2, dtype=jnp.int32)
    longitude = owners * WD + jnp.clip(offset + jitter_cols, 0, WD - 1)
    latitude = latitude.at[0, 0].set(0)
    longitude = longitude.at[0, 0].set(0)
    longitude = longitude.at[H - 1, W - 1].set(W - 1)
    return jnp.stack([latitude, longitude]).astype(jnp.int32)


def steps_of(own_key, dims, cuts, least, largest):
    def one(axis_at, blocks):
        steps = jax.random.uniform(jax.random.fold_in(jax.random.fold_in(own_key, 6), axis_at), (blocks,), jnp.float32, least / len(cuts), largest / len(cuts))
        return jnp.repeat(jnp.exp(steps), dims[axis_at] // blocks).reshape((-1,) + (1,) * (len(dims) - axis_at - 1))

    level = one(*cuts[0])
    for cut in cuts[1:]:
        level = level * one(*cut)
    return level


def noise(stream_key, dims, width, most, shards=(), kind=jnp.bfloat16):
    entries = jax.random.normal(stream_key, dims, jnp.float32) * width
    if len(shards) > 0:
        entries = steps_of(stream_key, dims, shards, -0.22, 0.18) * entries
    return jnp.clip(entries, min=-most, max=most).astype(kind)


def setup_inputs(seed: int = 0, part: int = 0) -> dict:
    splits = jax.random.split(jax.random.key(seed), 10)
    part_keys = jax.random.split(jax.random.fold_in(splits[9], part), 10)
    return {
        "latlon_fields": noise(part_keys[0], (CIN, NLAT, W), 1.0, 6.0, ((1, 16),)),
        "remap_table": draw_remap_table(jax.random.fold_in(splits[9], 71), part),
        "kernel_first": noise(splits[2], (3, 3, C, CIN), (9 * CIN) ** -0.5, 0.5),
        "kernel_second": noise(splits[3], (3, 3, C, C), (9 * C) ** -0.5, 0.25),
        "kernel_down": noise(splits[4], (3, 3, C2, C), (9 * C) ** -0.5, 0.25),
        "kernel_coarse": noise(splits[5], (3, 3, C2, C2), (9 * C2) ** -0.5, 0.1875),
        "kernel_up": noise(splits[6], (3, 3, C, C2), (9 * C2 // 4) ** -0.5, 0.375),
        "kernel_merge": noise(splits[7], (3, 3, C, 2 * C), (18 * C) ** -0.5, 0.1875),
        "projection": noise(splits[8], (COUT, C), C ** -0.5, 0.75),
    }


def extend_full(field_in):
    half = field_in.shape[2] // 2
    top_row = jnp.roll(field_in[:, :1], half, axis=2)
    bottom_row = jnp.zeros_like(field_in[:, :1])
    tall = jnp.concatenate([top_row, field_in, bottom_row], axis=1)
    return jnp.concatenate([tall[:, :, -1:], tall, tall[:, :, :1]], axis=2)


def convolve(extended, kernel, stride):
    channels = extended.shape[0]
    out_rows = (extended.shape[1] - 2) // stride
    out_cols = (extended.shape[2] - 2) // stride
    source = extended.astype(jnp.float32)
    weights = kernel.astype(jnp.float32)
    total = jnp.zeros((kernel.shape[2], out_rows, out_cols), jnp.float32)
    for row_tap in range(3):
        for col_tap in range(3):
            piece = lax.slice(source, (0, row_tap, col_tap),
                              (channels, row_tap + (out_rows - 1) * stride + 1, col_tap + (out_cols - 1) * stride + 1),
                              (1, stride, stride))
            total = total + jnp.einsum("oc,chw->ohw", weights[row_tap, col_tap], piece,
                                       precision=lax.Precision.HIGHEST)
    return total


def activate(values):
    return jax.nn.silu(values).astype(jnp.bfloat16)


def reference(latlon_fields, remap_table, kernel_first, kernel_second, kernel_down, kernel_coarse, kernel_up, kernel_merge, projection):
    remapped = latlon_fields[:, remap_table[0], remap_table[1]]
    first = activate(convolve(extend_full(remapped), kernel_first, 1))
    second = activate(convolve(extend_full(first), kernel_second, 1))
    coarse_in = activate(convolve(extend_full(second), kernel_down, 2))
    coarse_out = activate(convolve(extend_full(coarse_in), kernel_coarse, 1))
    grid_rows = second.shape[1]
    grid_cols = second.shape[2]
    stuffed = jnp.zeros((coarse_out.shape[0], grid_rows, grid_cols), jnp.float32)
    stuffed = stuffed.at[:, ::2, ::2].set(coarse_out.astype(jnp.float32))
    padded = jnp.pad(stuffed, ((0, 0), (1, 1), (0, 0)))
    padded = jnp.concatenate([padded[:, :, -1:], padded, padded[:, :, :1]], axis=2)
    lifted = convolve(padded, kernel_up, 1)
    upsampled = activate(lifted)
    joined = jnp.concatenate([second, upsampled], axis=0)
    merged = activate(convolve(extend_full(joined), kernel_merge, 1))
    count_out = projection.shape[0]
    update = jnp.einsum("oc,chw->ohw", projection.astype(jnp.float32), merged.astype(jnp.float32),
                        precision=lax.Precision.HIGHEST)
    return remapped[:count_out].astype(jnp.float32) + update
```

```python
import functools

import jax
import jax.numpy as jnp
from jax import lax
from jax.experimental import pallas as pl
from jax.experimental.pallas import tpu as pltpu
from jax.sharding import PartitionSpec as P

MESH = pl.DeviceIdType.MESH
F32 = jnp.float32
BF16 = jnp.bfloat16
HALO = 8
POLE = 8
OFFSETS = (0, 1, 2, -1)
NT = (((1,), (1,)), ((), ()))


def dot_nt(a, b):
    return lax.dot_general(a, b, NT, preferred_element_type=F32)


def silu(x):
    half = 0.5 * x
    return half * jnp.tanh(half) + half


def exchange_kernel(n, lat_ref, tab_ref, own_ref, left_ref, right_ref, anti_ref, recv, send_sem, recv_sem, own_sem, hsend, hrecv):
    me = lax.axis_index("lon")
    group = lax.axis_index("groups")
    cols = recv.shape[2]
    height = tab_ref.shape[1]
    channels = own_ref.shape[1]
    sub_rows = lat_ref.shape[0] // channels
    barrier = pltpu.get_barrier_semaphore()

    def greet(d, carry):
        pl.semaphore_signal(barrier, inc=1, device_id=(group, lax.rem(me + d, n)), device_id_type=MESH)
        return carry

    lax.fori_loop(1, n, greet, 0)
    mine = pltpu.make_async_copy(lat_ref.at[:, pl.ds(pl.multiple_of(me * cols, cols), cols)], recv.at[me], own_sem)
    mine.start()
    pl.semaphore_wait(barrier, n - 1)

    def block_copy(d, slot):
        target = lax.rem(me + d, n)
        return pltpu.make_async_remote_copy(
            src_ref=lat_ref.at[:, pl.ds(pl.multiple_of(target * cols, cols), cols)],
            dst_ref=recv.at[slot],
            send_sem=send_sem.at[d - 1],
            recv_sem=recv_sem.at[d - 1],
            device_id=(group, target),
            device_id_type=MESH,
        )

    def send(d, carry):
        block_copy(d, me).start()
        return carry

    lax.fori_loop(1, n, send, 0)

    p = lax.broadcasted_iota(jnp.int32, (cols, cols), 1)
    w = lax.broadcasted_iota(jnp.int32, (cols, cols), 0)
    half = cols // 2
    perm = (w == jnp.where(p < half, 2 * p, 2 * p - cols + 1)).astype(F32).astype(BF16)
    rows_at = jnp.dot(tab_ref[0].astype(F32).astype(BF16), perm, preferred_element_type=F32).astype(jnp.int32)
    cols_at = jnp.dot((tab_ref[1] - me * cols).astype(F32).astype(BF16), perm, preferred_element_type=F32).astype(jnp.int32)

    mine.wait()

    def receive(d, carry):
        block_copy(d, lax.rem(me - d + n, n)).wait_recv()
        return carry

    lax.fori_loop(1, n, receive, 0)

    at_col = lax.broadcasted_iota(jnp.int32, (cols, cols), 0)
    source = recv[...].reshape(n * lat_ref.shape[0], cols)
    chunk = 512
    total = source.shape[0]
    for h in range(0, height, 2):
        hot = jnp.concatenate(
            [(at_col == cols_at[h + q : h + q + 1]).astype(F32).astype(BF16) for q in range(2)], axis=1
        )
        row_sel = jnp.concatenate([rows_at[h : h + 1], rows_at[h + 1 : h + 2]], axis=1)
        picked = jnp.zeros((channels, 2 * cols), F32)
        for c0 in range(0, total, chunk):
            size = min(chunk, total - c0)
            got = jnp.dot(source[c0 : c0 + size], hot, preferred_element_type=F32)
            for r in range(size // channels):
                picked = jnp.where(row_sel == c0 // channels + r, got[r * channels : (r + 1) * channels], picked)
        for q in range(2):
            own_ref[h + q] = picked[:, q * cols : (q + 1) * cols].astype(BF16)

    def halo(k, src, dst, shift):
        return pltpu.make_async_remote_copy(
            src_ref=src, dst_ref=dst, send_sem=hsend.at[k], recv_sem=hrecv.at[k],
            device_id=(group, lax.rem(me + shift + 2 * n, n)), device_id_type=MESH)

    top = own_ref.at[pl.ds(0, POLE)]
    copies = [
        halo(0, own_ref, left_ref, 1),
        halo(1, own_ref, right_ref, -1),
        halo(2, top, anti_ref.at[0], n // 2),
        halo(3, top, anti_ref.at[1], n // 2 + 1),
        halo(4, top, anti_ref.at[2], n // 2 - 1),
    ]
    for c in copies:
        c.start()

    def sent(d, carry):
        block_copy(d, me).wait_send()
        return carry

    lax.fori_loop(1, n, sent, 0)
    for c in copies:
        c.wait()


def unet_kernel(own_ref, left_ref, right_ref, anti_ref, k1, k2, kd, kc, ku, km, kp, out_ref,
                xf, x1, x2, x3, xc, xu, w1, w2, wd, wc, wu, wma, wmb, wp):
    height, channels, cols = own_ref.shape
    half = cols // 2
    J = half + 2 * HALO
    C = k1.shape[2]
    C2 = kd.shape[2]
    COUT = kp.shape[0]
    pairs = height // 2
    AB = pairs + 1

    for w in (w1, w2, wd, wc, wu, wma, wmb, wp):
        w[...] = jnp.zeros_like(w)

    def fill(w, kernel, cin, first_in):
        for q in range(2):
            for p in range(2):
                for a in range(4):
                    for l, off in enumerate(OFFSETS):
                        kr, kcol = a - q, off - p + 1
                        if 0 <= kr < 3 and 0 <= kcol < 3:
                            at = (q * 2 + p) * C
                            lane = a * 4 * cin + l * cin
                            w[at : at + C, lane : lane + cin] = kernel[kr, kcol][:, first_in : first_in + cin]

    fill(w1, k1, channels, 0)
    fill(w2, k2, C, 0)
    fill(wma, km, C, 0)
    fill(wmb, km, C, C)
    for a in range(3):
        for l, kcol in ((0, 1), (1, 2), (3, 0)):
            wd[:, a * 4 * C + l * C : a * 4 * C + (l + 1) * C] = kd[a, kcol]
        for s, kcol in enumerate((1, 2, 0)):
            wc[:, (a * 3 + s) * C2 : (a * 3 + s + 1) * C2] = kc[a, kcol]
    for q, rows in ((0, ((0, 1),)), (1, ((0, 0), (1, 2)))):
        for p, columns in ((0, ((0, 1),)), (1, ((0, 0), (1, 2)))):
            at = (q * 2 + p) * C
            for ri, kr in rows:
                for ci, kcol in columns:
                    lane = (ri * 2 + ci) * C2
                    wu[at : at + C, lane : lane + C2] = ku[kr, kcol]
    for g in range(4):
        wp[g * COUT : (g + 1) * COUT, g * C : (g + 1) * C] = kp[...].astype(F32)

    def spread(g, l, r):
        lane = lax.broadcasted_iota(jnp.int32, g.shape, 1)
        even = jnp.where(lane < half, g, jnp.where(lane < half + HALO, pltpu.roll(r, half, 1), pltpu.roll(l, 2 * HALO, 1)))
        odd = jnp.where(lane < half, pltpu.roll(g, half, 1),
                        jnp.where(lane < half + HALO, r, pltpu.roll(l, half + 2 * HALO, 1)))
        after = jnp.where(lane == J - 1, pltpu.roll(even, J - 1, 1), pltpu.roll(even, cols - 1, 1))
        before = jnp.where(lane == 0, pltpu.roll(odd, cols - J + 1, 1), pltpu.roll(odd, 1, 1))
        return jnp.concatenate([even, odd, after, before], axis=0)

    tap = 4 * channels

    def put(slot, value):
        i, a = slot // 2, slot % 2
        if i < xf.shape[0]:
            xf[i, :, a * tap : (a + 1) * tap] = value
        if i > 0:
            xf[i - 1, :, (a + 2) * tap : (a + 3) * tap] = value

    for h in range(height):
        value = spread(own_ref[h].astype(F32), left_ref[h].astype(F32), right_ref[h].astype(F32)).T[:J].astype(BF16)
        put(h + 1, value)
        if h == 0:
            put(height + 2, value)
    for h in range(POLE - 1):
        value = spread(anti_ref[0, h].astype(F32), anti_ref[1, h].astype(F32), anti_ref[2, h].astype(F32)).T[:J].astype(BF16)
        put(height + 3 + h, value)
        if h == 0:
            put(0, value)
    put(height + 1, jnp.zeros((J, tap), BF16))

    def neighbours(v):
        count = v.shape[0]
        v = v.reshape(count // J, J, v.shape[1])
        lane = lax.broadcasted_iota(jnp.int32, v.shape, 2)
        other = jnp.where(lane < C, pltpu.roll(v, J - 1, 1), pltpu.roll(v, 1, 1))
        return jnp.concatenate([v, other], axis=2).astype(BF16)

    def store_pair(x, i0, count, s):
        x[pl.ds(i0, count), 1] = neighbours(s[:, : 2 * C])
        x[pl.ds(i0 + 1, count), 0] = neighbours(s[:, 2 * C :])

    def wrap(x):
        x[0, 0] = x[AB, 1]
        x[AB, 0] = x[0, 1]
        x[AB - 1, 1] = jnp.zeros(x.shape[2:], BF16)

    def taps(x, i0, count, a, width):
        v = x[pl.ds(i0 + a // 2, count), a % 2, 0:width]
        return v.reshape(count * width, v.shape[-1])

    def own_loop(steps, body):
        def run(t, carry):
            body(t)
            return carry
        lax.fori_loop(0, steps, run, 0)

    B = 4

    def first(i0, count):
        store_pair(x1, i0, count, silu(dot_nt(xf[pl.ds(i0, count)].reshape(count * J, 4 * tap), w1[...])))

    first(AB, 3)
    own_loop(pairs // B, lambda t: first(t * B, B))
    wrap(x1)

    def second(i0, count):
        acc = dot_nt(taps(x1, i0, count, 0, J), w2[:, : 4 * C])
        for a in range(1, 4):
            acc += dot_nt(taps(x1, i0, count, a, J), w2[:, a * 4 * C : (a + 1) * 4 * C])
        store_pair(x2, i0, count, silu(acc))

    second(AB, 2)
    own_loop(pairs // B, lambda t: second(t * B, B))
    wrap(x2)

    def shifts(v, both):
        v = v.reshape(v.shape[0] // J, J, v.shape[1])
        parts = [v, pltpu.roll(v, J - 1, 1)]
        if both:
            parts.append(pltpu.roll(v, 1, 1))
        return jnp.concatenate(parts, axis=2).astype(BF16)

    def down(i0, slot, count):
        acc = dot_nt(taps(x2, i0, count, 0, J), wd[:, : 4 * C])
        for a in range(1, 3):
            acc += dot_nt(taps(x2, i0, count, a, J), wd[:, a * 4 * C : (a + 1) * 4 * C])
        xc[pl.ds(slot, count)] = shifts(silu(acc), True)

    down(AB, pairs + 3, 2)
    own_loop(pairs // B, lambda t: down(t * B, t * B + 1, B))
    xc[0] = xc[pairs + 3]
    xc[pairs + 2] = xc[1]
    xc[pairs + 1] = jnp.zeros(xc.shape[1:], BF16)

    def coarse(i0, slot, count):
        acc = None
        for a in range(3):
            v = xc[pl.ds(i0 + a, count)].reshape(count * J, 3 * C2)
            part = dot_nt(v, wc[:, a * 3 * C2 : (a + 1) * 3 * C2])
            acc = part if acc is None else acc + part
        xu[pl.ds(slot, count)] = shifts(silu(acc), False)

    coarse(pairs + 2, pairs + 1, 1)
    own_loop(pairs // B, lambda t: coarse(t * B, t * B, B))
    xu[pairs] = jnp.zeros(xu.shape[1:], BF16)

    def up(i0, count):
        acc = dot_nt(xu[pl.ds(i0, count)].reshape(count * J, 2 * C2), wu[:, : 2 * C2])
        return silu(acc + dot_nt(xu[pl.ds(i0 + 1, count)].reshape(count * J, 2 * C2), wu[:, 2 * C2 :]))

    def up_own(t):
        store_pair(x3, t * B, B, up(t * B, B))

    own_loop(pairs // B, up_own)
    v = xu[pairs + 1]
    x3[0, 0] = neighbours(silu(dot_nt(v, wu[0 : 2 * C, : 2 * C2])))[0]
    x3[AB - 1, 1] = jnp.zeros(x3.shape[2:], BF16)

    p = lax.broadcasted_iota(jnp.int32, (cols, cols), 0)
    w = lax.broadcasted_iota(jnp.int32, (cols, cols), 1)
    unperm = (w == jnp.where(p < half, 2 * p, 2 * p - cols + 1)).astype(F32)
    wpb = wp[...].astype(BF16)

    for t in range(pairs // B):
        i0 = t * B
        acc = None
        for a in range(4):
            for x, w in ((x2, wma), (x3, wmb)):
                part = dot_nt(taps(x, i0, B, a, half), w[:, a * 4 * C : (a + 1) * 4 * C])
                acc = part if acc is None else acc + part
        merged = silu(acc).astype(BF16)
        update = dot_nt(wpb, merged)
        lines = []
        for b in range(B):
            u = update[:, b * half : (b + 1) * half]
            for q in range(2):
                line = jnp.concatenate([u[2 * q * COUT : (2 * q + 1) * COUT], u[(2 * q + 1) * COUT : (2 * q + 2) * COUT]], axis=1)
                lines.append(line + own_ref[2 * (i0 + b) + q].astype(F32)[:COUT])
        woven = jnp.dot(jnp.concatenate(lines, axis=0), unperm, precision=lax.Precision.HIGHEST, preferred_element_type=F32)
        for m in range(2 * B):
            out_ref[:, 2 * i0 + m, :] = woven[m * COUT : (m + 1) * COUT]


def shards(latlon, table, k1, k2, kd, kc, ku, km, kp):
    n = lax.axis_size("lon")
    channels, sub_rows, width = latlon.shape
    height, cols = table.shape[1], table.shape[2]
    lat = jnp.swapaxes(latlon, 0, 1).reshape(sub_rows * channels, width)
    vm = pl.BlockSpec(memory_space=pltpu.VMEM)
    field = jax.ShapeDtypeStruct((height, channels, cols), BF16)
    own, left, right, anti = pl.pallas_call(
        functools.partial(exchange_kernel, n),
        out_shape=(field, field, field, jax.ShapeDtypeStruct((3, POLE, channels, cols), BF16)),
        in_specs=[vm] * 2,
        out_specs=(vm,) * 4,
        scratch_shapes=[
            pltpu.VMEM((n, sub_rows * channels, cols), BF16),
            pltpu.SemaphoreType.DMA((n - 1,)),
            pltpu.SemaphoreType.DMA((n - 1,)),
            pltpu.SemaphoreType.DMA,
            pltpu.SemaphoreType.DMA((5,)),
            pltpu.SemaphoreType.DMA((5,)),
        ],
        compiler_params=pltpu.CompilerParams(collective_id=0, has_side_effects=True, vmem_limit_bytes=48 * 2**20),
        name="exchange",
    )(lat, table)
    C, C2, COUT = k1.shape[2], kd.shape[2], kp.shape[0]
    J = cols // 2 + 2 * HALO
    pairs = height // 2
    return pl.pallas_call(
        unet_kernel,
        out_shape=jax.ShapeDtypeStruct((COUT, height, cols), F32),
        in_specs=[vm] * 11,
        out_specs=vm,
        scratch_shapes=[
            pltpu.VMEM((pairs + 4, J, 16 * channels), BF16),
            pltpu.VMEM((pairs + 5, 2, J, 4 * C), BF16),
            pltpu.VMEM((pairs + 4, 2, J, 4 * C), BF16),
            pltpu.VMEM((pairs + 1, 2, J, 4 * C), BF16),
            pltpu.VMEM((pairs + 5, J, 3 * C2), BF16),
            pltpu.VMEM((pairs + 2, J, 2 * C2), BF16),
            pltpu.VMEM((4 * C, 16 * channels), BF16),
            pltpu.VMEM((4 * C, 16 * C), BF16),
            pltpu.VMEM((C2, 12 * C), BF16),
            pltpu.VMEM((C2, 9 * C2), BF16),
            pltpu.VMEM((4 * C, 4 * C2), BF16),
            pltpu.VMEM((4 * C, 16 * C), BF16),
            pltpu.VMEM((4 * C, 16 * C), BF16),
            pltpu.VMEM((4 * COUT, 4 * C), F32),
        ],
        compiler_params=pltpu.CompilerParams(vmem_limit_bytes=48 * 2**20),
        name="unet",
    )(own, left, right, anti, k1, k2, kd, kc, ku, km, kp)


def solution(mesh):
    return jax.shard_map(
        shards,
        mesh=mesh,
        in_specs=(P("groups", "lon", None), P(None, None, "lon")) + (P(),) * 7,
        out_specs=P("groups", None, "lon"),
        check_vma=False,
    )
```

```python
import functools

import jax
import jax.numpy as jnp
from jax import lax
from jax.experimental import pallas as pl
from jax.experimental.pallas import tpu as pltpu
from jax.sharding import PartitionSpec as P

MESH = pl.DeviceIdType.MESH
F32 = jnp.float32
BF16 = jnp.bfloat16
HALO = 8
PER = 8
OFFSETS = (0, 1, 2, -1)
NT = (((1,), (1,)), ((), ()))


def dot_nt(a, b):
    return lax.dot_general(a, b, NT, preferred_element_type=F32)


def silu(x):
    half = 0.5 * x
    return half * jnp.tanh(half) + half


def exchange_kernel(n, lat_ref, tab_ref, own_ref, left_ref, right_ref, anti_ref, anti_left_ref, anti_right_ref,
                    recv, edge, send_sem, recv_sem, own_sem, hsend, hrecv):
    me = lax.axis_index("lon")
    group = lax.axis_index("groups")
    cols = recv.shape[2]
    height = tab_ref.shape[1]
    per = height // own_ref.shape[0]
    channels = own_ref.shape[2] // per
    barrier = pltpu.get_barrier_semaphore()

    def greet(d, carry):
        pl.semaphore_signal(barrier, inc=1, device_id=(group, lax.rem(me + d, n)), device_id_type=MESH)
        return carry

    lax.fori_loop(1, n, greet, 0)
    mine = pltpu.make_async_copy(lat_ref.at[:, pl.ds(pl.multiple_of(me * cols, cols), cols)], recv.at[me], own_sem)
    mine.start()
    pl.semaphore_wait(barrier, n - 1)

    def block_copy(d, slot):
        target = lax.rem(me + d, n)
        return pltpu.make_async_remote_copy(
            src_ref=lat_ref.at[:, pl.ds(pl.multiple_of(target * cols, cols), cols)],
            dst_ref=recv.at[slot],
            send_sem=send_sem.at[d - 1],
            recv_sem=recv_sem.at[d - 1],
            device_id=(group, target),
            device_id_type=MESH,
        )

    def send(d, carry):
        block_copy(d, me).start()
        return carry

    lax.fori_loop(1, n, send, 0)

    p = lax.broadcasted_iota(jnp.int32, (cols, cols), 0)
    w = lax.broadcasted_iota(jnp.int32, (cols, cols), 1)
    half = cols // 2
    perm = (w == jnp.where(p < half, 2 * p, 2 * p - cols + 1)).astype(F32).astype(BF16)
    rows_at = dot_nt(perm, tab_ref[0].astype(F32).astype(BF16)).astype(jnp.int32)
    cols_at = dot_nt(perm, (tab_ref[1] - me * cols).astype(F32).astype(BF16)).astype(jnp.int32)
    wide = per * channels
    lane = lax.broadcasted_iota(jnp.int32, (cols, wide), 1)
    hots = [(cols_at[:, h : h + 1] == w).astype(F32).astype(BF16) for h in range(height)]
    at_row = [jnp.broadcast_to(rows_at[:, h : h + 1], (cols, wide)) - lane // channels for h in range(height)]
    fi = lax.broadcasted_iota(jnp.int32, (per * wide, wide), 0)
    fo = lax.broadcasted_iota(jnp.int32, (per * wide, wide), 1)
    fold = ((fi // wide == fo // channels) & (fi % channels == fo % channels)).astype(F32).astype(BF16)

    mine.wait()

    def receive(d, carry):
        block_copy(d, lax.rem(me - d + n, n)).wait_recv()
        return carry

    lax.fori_loop(1, n, receive, 0)

    source = recv[...].reshape(n * lat_ref.shape[0], cols)
    tiles = source.shape[0] // wide
    for g in range(own_ref.shape[0]):
        got = dot_nt(jnp.concatenate(hots[g * per : (g + 1) * per], axis=0), source)
        picked = []
        for q in range(per):
            one = jnp.zeros((cols, wide), F32)
            for t in range(tiles):
                value = got[q * cols : (q + 1) * cols, t * wide : (t + 1) * wide]
                one = jnp.where(at_row[g * per + q] == t * per, value, one)
            picked.append(one.astype(BF16))
        block = jnp.dot(jnp.concatenate(picked, axis=1), fold, preferred_element_type=F32)
        own_ref[g] = block.astype(BF16)
        edge[0, g] = jnp.concatenate([block[0:HALO], block[half : half + HALO]], axis=0).astype(BF16)
        edge[1, g] = jnp.concatenate([block[half - HALO : half], block[cols - HALO : cols]], axis=0).astype(BF16)

    def halo(k, src, dst, shift):
        return pltpu.make_async_remote_copy(
            src_ref=src, dst_ref=dst, send_sem=hsend.at[k], recv_sem=hrecv.at[k],
            device_id=(group, lax.rem(me + shift + 2 * n, n)), device_id_type=MESH)

    copies = [
        halo(0, own_ref.at[0], anti_ref, n // 2),
        halo(1, edge.at[1], left_ref, 1),
        halo(2, edge.at[0], right_ref, -1),
        halo(3, edge.at[1, 0], anti_left_ref, n // 2 + 1),
        halo(4, edge.at[0, 0], anti_right_ref, n // 2 - 1),
    ]
    for c in copies:
        c.start()

    def sent(d, carry):
        block_copy(d, me).wait_send()
        return carry

    lax.fori_loop(1, n, sent, 0)
    for c in copies:
        c.wait()


def unet_kernel(own_ref, left_ref, right_ref, anti_ref, anti_left_ref, anti_right_ref, k1, k2, kd, kc, ku, km, kp, out_ref,
                xf, x1, x2, x3, xc, xu, w1, wlast, wfirst, wnext, w2, wd, wc, wu, wma, wmb, wp):
    groups, cols, wide = own_ref.shape
    height = groups * PER
    channels = wide // PER
    half = cols // 2
    J = half + 2 * HALO
    C = k1.shape[2]
    C2 = kd.shape[2]
    COUT = kp.shape[0]
    pairs = height // 2
    AB = pairs + 1

    for w in (w1, wlast, wfirst, wnext, w2, wd, wc, wu, wma, wmb, wp):
        w[...] = jnp.zeros_like(w)

    def fill(w, kernel, cin, first_in):
        for q in range(2):
            for p in range(2):
                for a in range(4):
                    for l, off in enumerate(OFFSETS):
                        kr, kcol = a - q, off - p + 1
                        if 0 <= kr < 3 and 0 <= kcol < 3:
                            at = (q * 2 + p) * C
                            lane = a * 4 * cin + l * cin
                            w[at : at + C, lane : lane + cin] = kernel[kr, kcol][:, first_in : first_in + cin]

    for p in range(2):
        for l, off in enumerate(OFFSETS):
            if not 0 <= off - p + 1 < 3:
                continue
            k = [k1[kr, off - p + 1] for kr in range(3)]
            lane = l * wide
            for r in range(PER):
                at = (r * 2 + p) * C
                for kr in range(3):
                    if 0 <= r + kr - 1 < PER:
                        to = lane + (r + kr - 1) * channels
                        w1[at : at + C, to : to + channels] = k[kr]
            end = lane + (PER - 1) * channels
            wlast[p * C : (p + 1) * C, end : end + channels] = k[0]
            wfirst[p * C : (p + 1) * C, lane : lane + channels] = k[0]
            wnext[p * C : (p + 1) * C, lane : lane + channels] = k[2]
    fill(w2, k2, C, 0)
    fill(wma, km, C, 0)
    fill(wmb, km, C, C)
    for a in range(3):
        for l, kcol in ((0, 1), (1, 2), (3, 0)):
            wd[:, a * 4 * C + l * C : a * 4 * C + (l + 1) * C] = kd[a, kcol]
        for s, kcol in enumerate((1, 2, 0)):
            wc[:, (a * 3 + s) * C2 : (a * 3 + s + 1) * C2] = kc[a, kcol]
    for q, rows in ((0, ((0, 1),)), (1, ((0, 0), (1, 2)))):
        for p, columns in ((0, ((0, 1),)), (1, ((0, 0), (1, 2)))):
            at = (q * 2 + p) * C
            for ri, kr in rows:
                for ci, kcol in columns:
                    lane = (ri * 2 + ci) * C2
                    wu[at : at + C, lane : lane + C2] = ku[kr, kcol]
    for g in range(4):
        wp[g * COUT : (g + 1) * COUT, g * C : (g + 1) * C] = kp[...].astype(F32)

    def spread(g, l, r):
        even = jnp.concatenate([g[:half], r[:HALO], l[:HALO]], axis=0)
        odd = jnp.concatenate([g[half:], r[HALO:], l[HALO:]], axis=0)
        return jnp.concatenate([even, odd, pltpu.roll(even, J - 1, 0), pltpu.roll(odd, 1, 0)], axis=1).astype(BF16)

    for g in range(groups):
        xf[g] = spread(own_ref[g].astype(F32), left_ref[g].astype(F32), right_ref[g].astype(F32))
    xf[groups] = spread(anti_ref[...].astype(F32), anti_left_ref[...].astype(F32), anti_right_ref[...].astype(F32))

    def neighbours(v):
        count = v.shape[0]
        v = v.reshape(count // J, J, v.shape[1])
        lane = lax.broadcasted_iota(jnp.int32, v.shape, 2)
        other = jnp.where(lane < C, pltpu.roll(v, J - 1, 1), pltpu.roll(v, 1, 1))
        return jnp.concatenate([v, other], axis=2).astype(BF16)

    def store_pair(x, i0, count, s):
        x[pl.ds(i0, count), 1] = neighbours(s[:, : 2 * C])
        x[pl.ds(i0 + 1, count), 0] = neighbours(s[:, 2 * C :])

    def wrap(x):
        x[0, 0] = x[AB, 1]
        x[AB, 0] = x[0, 1]
        x[AB - 1, 1] = jnp.zeros(x.shape[2:], BF16)

    def taps(x, i0, count, a, width):
        v = x[pl.ds(i0 + a // 2, count), a % 2, 0:width]
        return v.reshape(count * width, v.shape[-1])

    B = pairs

    def own_loop(steps, body):
        for t in range(steps):
            body(t)

    every = groups + 1
    acc = dot_nt(xf[...].reshape(every * J, 4 * wide), w1[...]).reshape(every, J, PER * 2 * C)
    from_last = dot_nt(xf[pl.ds(0, groups - 1)].reshape((groups - 1) * J, 4 * wide), wlast[...]).reshape(groups - 1, J, 2 * C)
    from_next = dot_nt(xf[pl.ds(1, groups - 1)].reshape((groups - 1) * J, 4 * wide), wnext[...]).reshape(groups - 1, J, 2 * C)
    own_top = dot_nt(xf[groups], wfirst[...])
    anti_top = dot_nt(xf[0], wfirst[...])
    for g in range(every):
        for r in range(PER):
            v = acc[g, :, r * 2 * C : (r + 1) * 2 * C]
            if r == 0:
                v = v + (anti_top if g == groups else own_top if g == 0 else from_last[g - 1])
            if r == PER - 1 and g < groups - 1:
                v = v + from_next[g]
            slot = g * PER + r + 1 + (2 if g == groups else 0)
            if slot // 2 < x1.shape[0]:
                x1[slot // 2, slot % 2] = neighbours(silu(v))[0]
    wrap(x1)

    def second(i0, count):
        acc = dot_nt(taps(x1, i0, count, 0, J), w2[:, : 4 * C])
        for a in range(1, 4):
            acc += dot_nt(taps(x1, i0, count, a, J), w2[:, a * 4 * C : (a + 1) * 4 * C])
        store_pair(x2, i0, count, silu(acc))

    second(AB, 2)
    own_loop(pairs // B, lambda t: second(t * B, B))
    wrap(x2)

    def shifts(v, both):
        v = v.reshape(v.shape[0] // J, J, v.shape[1])
        parts = [v, pltpu.roll(v, J - 1, 1)]
        if both:
            parts.append(pltpu.roll(v, 1, 1))
        return jnp.concatenate(parts, axis=2).astype(BF16)

    def down(i0, slot, count):
        acc = dot_nt(taps(x2, i0, count, 0, J), wd[:, : 4 * C])
        for a in range(1, 3):
            acc += dot_nt(taps(x2, i0, count, a, J), wd[:, a * 4 * C : (a + 1) * 4 * C])
        xc[pl.ds(slot, count)] = shifts(silu(acc), True)

    down(AB, pairs + 3, 2)
    own_loop(pairs // B, lambda t: down(t * B, t * B + 1, B))
    xc[0] = xc[pairs + 3]
    xc[pairs + 2] = xc[1]
    xc[pairs + 1] = jnp.zeros(xc.shape[1:], BF16)

    def coarse(i0, slot, count):
        acc = None
        for a in range(3):
            v = xc[pl.ds(i0 + a, count)].reshape(count * J, 3 * C2)
            part = dot_nt(v, wc[:, a * 3 * C2 : (a + 1) * 3 * C2])
            acc = part if acc is None else acc + part
        xu[pl.ds(slot, count)] = shifts(silu(acc), False)

    coarse(pairs + 2, pairs + 1, 1)
    own_loop(pairs // B, lambda t: coarse(t * B, t * B, B))
    xu[pairs] = jnp.zeros(xu.shape[1:], BF16)

    def up(i0, count):
        acc = dot_nt(xu[pl.ds(i0, count)].reshape(count * J, 2 * C2), wu[:, : 2 * C2])
        return silu(acc + dot_nt(xu[pl.ds(i0 + 1, count)].reshape(count * J, 2 * C2), wu[:, 2 * C2 :]))

    def up_own(t):
        store_pair(x3, t * B, B, up(t * B, B))

    own_loop(pairs // B, up_own)
    v = xu[pairs + 1]
    x3[0, 0] = neighbours(silu(dot_nt(v, wu[0 : 2 * C, : 2 * C2])))[0]
    x3[AB - 1, 1] = jnp.zeros(x3.shape[2:], BF16)

    p = lax.broadcasted_iota(jnp.int32, (cols, cols), 0)
    w = lax.broadcasted_iota(jnp.int32, (cols, cols), 1)
    unperm = (w == jnp.where(p < half, 2 * p, 2 * p - cols + 1)).astype(F32)
    wpb = wp[...].astype(BF16)

    for t in range(pairs // B):
        i0 = t * B
        acc = None
        for a in range(4):
            for x, w in ((x2, wma), (x3, wmb)):
                part = dot_nt(taps(x, i0, B, a, half), w[:, a * 4 * C : (a + 1) * 4 * C])
                acc = part if acc is None else acc + part
        merged = silu(acc).astype(BF16)
        update = dot_nt(wpb, merged)
        lines = []
        plain = [own_ref[g].astype(F32).T for g in range(groups)]
        for b in range(B):
            u = update[:, b * half : (b + 1) * half]
            for q in range(2):
                line = jnp.concatenate([u[2 * q * COUT : (2 * q + 1) * COUT], u[(2 * q + 1) * COUT : (2 * q + 2) * COUT]], axis=1)
                h = 2 * (i0 + b) + q
                at = (h % PER) * channels
                lines.append(line + plain[h // PER][at : at + COUT])
        woven = jnp.dot(jnp.concatenate(lines, axis=0), unperm, precision=lax.Precision.HIGHEST, preferred_element_type=F32)
        for m in range(2 * B):
            out_ref[:, 2 * i0 + m, :] = woven[m * COUT : (m + 1) * COUT]


def shards(latlon, table, k1, k2, kd, kc, ku, km, kp):
    n = lax.axis_size("lon")
    channels, sub_rows, width = latlon.shape
    height, cols = table.shape[1], table.shape[2]
    lat = jnp.swapaxes(latlon, 0, 1).reshape(sub_rows * channels, width)
    vm = pl.BlockSpec(memory_space=pltpu.VMEM)
    groups = height // PER
    edges = jax.ShapeDtypeStruct((groups, 2 * HALO, PER * channels), BF16)
    corner = jax.ShapeDtypeStruct((2 * HALO, PER * channels), BF16)
    remapped = pl.pallas_call(
        functools.partial(exchange_kernel, n),
        out_shape=(jax.ShapeDtypeStruct((groups, cols, PER * channels), BF16), edges, edges,
                   jax.ShapeDtypeStruct((cols, PER * channels), BF16), corner, corner),
        in_specs=[vm] * 2,
        out_specs=(vm,) * 6,
        scratch_shapes=[
            pltpu.VMEM((n, sub_rows * channels, cols), BF16),
            pltpu.VMEM((2, groups, 2 * HALO, PER * channels), BF16),
            pltpu.SemaphoreType.DMA((n - 1,)),
            pltpu.SemaphoreType.DMA((n - 1,)),
            pltpu.SemaphoreType.DMA,
            pltpu.SemaphoreType.DMA((5,)),
            pltpu.SemaphoreType.DMA((5,)),
        ],
        compiler_params=pltpu.CompilerParams(collective_id=0, has_side_effects=True, vmem_limit_bytes=48 * 2**20),
        name="exchange",
    )(lat, table)
    C, C2, COUT = k1.shape[2], kd.shape[2], kp.shape[0]
    J = cols // 2 + 2 * HALO
    pairs = height // 2
    return pl.pallas_call(
        unet_kernel,
        out_shape=jax.ShapeDtypeStruct((COUT, height, cols), F32),
        in_specs=[vm] * 13,
        out_specs=vm,
        scratch_shapes=[
            pltpu.VMEM((height // PER + 1, J, 4 * PER * channels), BF16),
            pltpu.VMEM((pairs + 5, 2, J, 4 * C), BF16),
            pltpu.VMEM((pairs + 4, 2, J, 4 * C), BF16),
            pltpu.VMEM((pairs + 1, 2, J, 4 * C), BF16),
            pltpu.VMEM((pairs + 5, J, 3 * C2), BF16),
            pltpu.VMEM((pairs + 2, J, 2 * C2), BF16),
            pltpu.VMEM((2 * C * PER, 4 * PER * channels), BF16),
            pltpu.VMEM((2 * C, 4 * PER * channels), BF16),
            pltpu.VMEM((2 * C, 4 * PER * channels), BF16),
            pltpu.VMEM((2 * C, 4 * PER * channels), BF16),
            pltpu.VMEM((4 * C, 16 * C), BF16),
            pltpu.VMEM((C2, 12 * C), BF16),
            pltpu.VMEM((C2, 9 * C2), BF16),
            pltpu.VMEM((4 * C, 4 * C2), BF16),
            pltpu.VMEM((4 * C, 16 * C), BF16),
            pltpu.VMEM((4 * C, 16 * C), BF16),
            pltpu.VMEM((4 * COUT, 4 * C), F32),
        ],
        compiler_params=pltpu.CompilerParams(vmem_limit_bytes=48 * 2**20),
        name="unet",
    )(*remapped, k1, k2, kd, kc, ku, km, kp)


def solution(mesh):
    return jax.shard_map(
        shards,
        mesh=mesh,
        in_specs=(P("groups", "lon", None), P(None, None, "lon")) + (P(),) * 7,
        out_specs=P("groups", None, "lon"),
        check_vma=False,
    )
```

```python
import functools

import jax
import jax.numpy as jnp
from jax import lax
from jax.experimental import pallas as pl
from jax.experimental.pallas import tpu as pltpu
from jax.sharding import PartitionSpec as P

MESH = pl.DeviceIdType.MESH
F32 = jnp.float32
BF16 = jnp.bfloat16
HALO = 8
PER = 8
OFFSETS = (0, 1, 2, -1)
NT = (((1,), (1,)), ((), ()))


def dot_nt(a, b):
    return lax.dot_general(a, b, NT, preferred_element_type=F32)


def silu(x):
    half = 0.5 * x
    return half * jnp.tanh(half) + half


def clear(*arrays):
    for w in arrays:
        w[...] = jnp.zeros_like(w)


def fill(w, kernel, cin, first_in):
    C = kernel.shape[2]
    for q in range(2):
        for p in range(2):
            for a in range(4):
                for l, off in enumerate(OFFSETS):
                    kr, kcol = a - q, off - p + 1
                    if 0 <= kr < 3 and 0 <= kcol < 3:
                        at = (q * 2 + p) * C
                        lane = a * 4 * cin + l * cin
                        w[at : at + C, lane : lane + cin] = kernel[kr, kcol][:, first_in : first_in + cin]


def fine_weights(k1, k2, km, w1, wlast, wfirst, wnext, w2, wma, wmb):
    C, channels = k1.shape[2], k1.shape[3]
    wide = PER * channels
    clear(w1, wlast, wfirst, wnext, w2, wma, wmb)
    for p in range(2):
        for l, off in enumerate(OFFSETS):
            if not 0 <= off - p + 1 < 3:
                continue
            k = [k1[kr, off - p + 1] for kr in range(3)]
            lane = l * wide
            for r in range(PER):
                at = (r * 2 + p) * C
                for kr in range(3):
                    if 0 <= r + kr - 1 < PER:
                        to = lane + (r + kr - 1) * channels
                        w1[at : at + C, to : to + channels] = k[kr]
            end = lane + (PER - 1) * channels
            wlast[p * C : (p + 1) * C, end : end + channels] = k[0]
            wfirst[p * C : (p + 1) * C, lane : lane + channels] = k[0]
            wnext[p * C : (p + 1) * C, lane : lane + channels] = k[2]
    fill(w2, k2, C, 0)
    fill(wma, km, C, 0)
    fill(wmb, km, C, C)


def coarse_weights(kd, kc, ku, kp, wd, wc, wu, wp):
    C2, C = kd.shape[2], kd.shape[3]
    COUT = kp.shape[0]
    clear(wd, wc, wu, wp)
    for a in range(3):
        for l, kcol in ((0, 1), (1, 2), (3, 0)):
            wd[:, a * 4 * C + l * C : a * 4 * C + (l + 1) * C] = kd[a, kcol]
        for s, kcol in enumerate((1, 2, 0)):
            wc[:, (a * 3 + s) * C2 : (a * 3 + s + 1) * C2] = kc[a, kcol]
    for q, rows in ((0, ((0, 1),)), (1, ((0, 0), (1, 2)))):
        for p, columns in ((0, ((0, 1),)), (1, ((0, 0), (1, 2)))):
            at = (q * 2 + p) * C
            for ri, kr in rows:
                for ci, kcol in columns:
                    lane = (ri * 2 + ci) * C2
                    wu[at : at + C, lane : lane + C2] = ku[kr, kcol]
    for g in range(4):
        wp[g * COUT : (g + 1) * COUT, g * C : (g + 1) * C] = kp[...].astype(F32)


def exchange_kernel(n, lat_ref, tab_ref, k1, k2, kd, kc, ku, km, kp,
                    own_ref, left_ref, right_ref, anti_ref, anti_left_ref, anti_right_ref,
                    w1, wlast, wfirst, wnext, w2, wd, wc, wu, wma, wmb, wp,
                    recv, edge, send_sem, recv_sem, own_sem, hsend, hrecv):
    me = lax.axis_index("lon")
    group = lax.axis_index("groups")
    cols = recv.shape[2]
    height = tab_ref.shape[1]
    per = height // own_ref.shape[0]
    channels = own_ref.shape[2] // per
    barrier = pltpu.get_barrier_semaphore()

    def greet(d, carry):
        pl.semaphore_signal(barrier, inc=1, device_id=(group, lax.rem(me + d, n)), device_id_type=MESH)
        return carry

    lax.fori_loop(1, n, greet, 0)
    mine = pltpu.make_async_copy(lat_ref.at[:, pl.ds(pl.multiple_of(me * cols, cols), cols)], recv.at[me], own_sem)
    mine.start()
    coarse_weights(kd, kc, ku, kp, wd, wc, wu, wp)
    pl.semaphore_wait(barrier, n - 1)

    def block_copy(d, slot):
        target = lax.rem(me + d, n)
        return pltpu.make_async_remote_copy(
            src_ref=lat_ref.at[:, pl.ds(pl.multiple_of(target * cols, cols), cols)],
            dst_ref=recv.at[slot],
            send_sem=send_sem.at[d - 1],
            recv_sem=recv_sem.at[d - 1],
            device_id=(group, target),
            device_id_type=MESH,
        )

    def send(d, carry):
        block_copy(d, me).start()
        return carry

    lax.fori_loop(1, n, send, 0)

    fine_weights(k1, k2, km, w1, wlast, wfirst, wnext, w2, wma, wmb)

    p = lax.broadcasted_iota(jnp.int32, (cols, cols), 0)
    w = lax.broadcasted_iota(jnp.int32, (cols, cols), 1)
    half = cols // 2
    perm = (w == jnp.where(p < half, 2 * p, 2 * p - cols + 1)).astype(F32).astype(BF16)
    rows_at = dot_nt(perm, tab_ref[0].astype(F32).astype(BF16)).astype(jnp.int32)
    cols_at = dot_nt(perm, (tab_ref[1] - me * cols).astype(F32).astype(BF16)).astype(jnp.int32)
    wide = per * channels
    lane = lax.broadcasted_iota(jnp.int32, (cols, wide), 1)
    hots = [(cols_at[:, h : h + 1] == w).astype(F32).astype(BF16) for h in range(height)]
    at_row = [jnp.broadcast_to(rows_at[:, h : h + 1], (cols, wide)) - lane // channels for h in range(height)]
    fi = lax.broadcasted_iota(jnp.int32, (per * wide, wide), 0)
    fo = lax.broadcasted_iota(jnp.int32, (per * wide, wide), 1)
    fold = ((fi // wide == fo // channels) & (fi % channels == fo % channels)).astype(F32).astype(BF16)

    mine.wait()

    def receive(d, carry):
        block_copy(d, lax.rem(me - d + n, n)).wait_recv()
        return carry

    lax.fori_loop(1, n, receive, 0)

    source = recv[...].reshape(n * lat_ref.shape[0], cols)
    tiles = source.shape[0] // wide
    for g in range(own_ref.shape[0]):
        got = dot_nt(jnp.concatenate(hots[g * per : (g + 1) * per], axis=0), source)
        picked = []
        for q in range(per):
            one = jnp.zeros((cols, wide), F32)
            for t in range(tiles):
                value = got[q * cols : (q + 1) * cols, t * wide : (t + 1) * wide]
                one = jnp.where(at_row[g * per + q] == t * per, value, one)
            picked.append(one.astype(BF16))
        block = jnp.dot(jnp.concatenate(picked, axis=1), fold, preferred_element_type=F32)
        own_ref[g] = block.astype(BF16)
        edge[0, g] = jnp.concatenate([block[0:HALO], block[half : half + HALO]], axis=0).astype(BF16)
        edge[1, g] = jnp.concatenate([block[half - HALO : half], block[cols - HALO : cols]], axis=0).astype(BF16)

    def halo(k, src, dst, shift):
        return pltpu.make_async_remote_copy(
            src_ref=src, dst_ref=dst, send_sem=hsend.at[k], recv_sem=hrecv.at[k],
            device_id=(group, lax.rem(me + shift + 2 * n, n)), device_id_type=MESH)

    copies = [
        halo(0, own_ref.at[0], anti_ref, n // 2),
        halo(1, edge.at[1], left_ref, 1),
        halo(2, edge.at[0], right_ref, -1),
        halo(3, edge.at[1, 0], anti_left_ref, n // 2 + 1),
        halo(4, edge.at[0, 0], anti_right_ref, n // 2 - 1),
    ]
    for c in copies:
        c.start()

    def sent(d, carry):
        block_copy(d, me).wait_send()
        return carry

    lax.fori_loop(1, n, sent, 0)
    for c in copies:
        c.wait()


def unet_kernel(own_ref, left_ref, right_ref, anti_ref, anti_left_ref, anti_right_ref,
                w1, wlast, wfirst, wnext, w2, wd, wc, wu, wma, wmb, wp, out_ref, xf, x1, x2, x3, xc, xu):
    groups, cols, wide = own_ref.shape
    height = groups * PER
    channels = wide // PER
    half = cols // 2
    J = half + 2 * HALO
    C = w2.shape[0] // 4
    C2 = wd.shape[0]
    COUT = wp.shape[0] // 4
    pairs = height // 2
    AB = pairs + 1

    def spread(g, l, r):
        even = jnp.concatenate([g[:half], r[:HALO], l[:HALO]], axis=0)
        odd = jnp.concatenate([g[half:], r[HALO:], l[HALO:]], axis=0)
        return jnp.concatenate([even, odd, pltpu.roll(even, J - 1, 0), pltpu.roll(odd, 1, 0)], axis=1).astype(BF16)

    for g in range(groups):
        xf[g] = spread(own_ref[g].astype(F32), left_ref[g].astype(F32), right_ref[g].astype(F32))
    xf[groups] = spread(anti_ref[...].astype(F32), anti_left_ref[...].astype(F32), anti_right_ref[...].astype(F32))

    def neighbours(v):
        count = v.shape[0]
        v = v.reshape(count // J, J, v.shape[1])
        lane = lax.broadcasted_iota(jnp.int32, v.shape, 2)
        other = jnp.where(lane < C, pltpu.roll(v, J - 1, 1), pltpu.roll(v, 1, 1))
        return jnp.concatenate([v, other], axis=2).astype(BF16)

    def store_pair(x, i0, count, s):
        x[pl.ds(i0, count), 1] = neighbours(s[:, : 2 * C])
        x[pl.ds(i0 + 1, count), 0] = neighbours(s[:, 2 * C :])

    def wrap(x):
        x[0, 0] = x[AB, 1]
        x[AB, 0] = x[0, 1]
        x[AB - 1, 1] = jnp.zeros(x.shape[2:], BF16)

    def taps(x, i0, count, a, width):
        v = x[pl.ds(i0 + a // 2, count), a % 2, 0:width]
        return v.reshape(count * width, v.shape[-1])

    B = pairs

    def own_loop(steps, body):
        for t in range(steps):
            body(t)

    every = groups + 1
    acc = dot_nt(xf[...].reshape(every * J, 4 * wide), w1[...]).reshape(every, J, PER * 2 * C)
    from_last = dot_nt(xf[pl.ds(0, groups - 1)].reshape((groups - 1) * J, 4 * wide), wlast[...]).reshape(groups - 1, J, 2 * C)
    from_next = dot_nt(xf[pl.ds(1, groups - 1)].reshape((groups - 1) * J, 4 * wide), wnext[...]).reshape(groups - 1, J, 2 * C)
    own_top = dot_nt(xf[groups], wfirst[...])
    anti_top = dot_nt(xf[0], wfirst[...])
    for g in range(every):
        for r in range(PER):
            v = acc[g, :, r * 2 * C : (r + 1) * 2 * C]
            if r == 0:
                v = v + (anti_top if g == groups else own_top if g == 0 else from_last[g - 1])
            if r == PER - 1 and g < groups - 1:
                v = v + from_next[g]
            slot = g * PER + r + 1 + (2 if g == groups else 0)
            if slot // 2 < x1.shape[0]:
                x1[slot // 2, slot % 2] = neighbours(silu(v))[0]
    wrap(x1)

    def second(i0, count):
        acc = dot_nt(taps(x1, i0, count, 0, J), w2[:, : 4 * C])
        for a in range(1, 4):
            acc += dot_nt(taps(x1, i0, count, a, J), w2[:, a * 4 * C : (a + 1) * 4 * C])
        store_pair(x2, i0, count, silu(acc))

    second(AB, 2)
    own_loop(pairs // B, lambda t: second(t * B, B))
    wrap(x2)

    def shifts(v, both):
        v = v.reshape(v.shape[0] // J, J, v.shape[1])
        parts = [v, pltpu.roll(v, J - 1, 1)]
        if both:
            parts.append(pltpu.roll(v, 1, 1))
        return jnp.concatenate(parts, axis=2).astype(BF16)

    def down(i0, slot, count):
        acc = dot_nt(taps(x2, i0, count, 0, J), wd[:, : 4 * C])
        for a in range(1, 3):
            acc += dot_nt(taps(x2, i0, count, a, J), wd[:, a * 4 * C : (a + 1) * 4 * C])
        xc[pl.ds(slot, count)] = shifts(silu(acc), True)

    down(AB, pairs + 3, 2)
    own_loop(pairs // B, lambda t: down(t * B, t * B + 1, B))
    xc[0] = xc[pairs + 3]
    xc[pairs + 2] = xc[1]
    xc[pairs + 1] = jnp.zeros(xc.shape[1:], BF16)

    def coarse(i0, slot, count):
        acc = None
        for a in range(3):
            v = xc[pl.ds(i0 + a, count)].reshape(count * J, 3 * C2)
            part = dot_nt(v, wc[:, a * 3 * C2 : (a + 1) * 3 * C2])
            acc = part if acc is None else acc + part
        xu[pl.ds(slot, count)] = shifts(silu(acc), False)

    coarse(pairs + 2, pairs + 1, 1)
    own_loop(pairs // B, lambda t: coarse(t * B, t * B, B))
    xu[pairs] = jnp.zeros(xu.shape[1:], BF16)

    def up(i0, count):
        acc = dot_nt(xu[pl.ds(i0, count)].reshape(count * J, 2 * C2), wu[:, : 2 * C2])
        return silu(acc + dot_nt(xu[pl.ds(i0 + 1, count)].reshape(count * J, 2 * C2), wu[:, 2 * C2 :]))

    def up_own(t):
        store_pair(x3, t * B, B, up(t * B, B))

    own_loop(pairs // B, up_own)
    v = xu[pairs + 1]
    x3[0, 0] = neighbours(silu(dot_nt(v, wu[0 : 2 * C, : 2 * C2])))[0]
    x3[AB - 1, 1] = jnp.zeros(x3.shape[2:], BF16)

    p = lax.broadcasted_iota(jnp.int32, (cols, cols), 0)
    w = lax.broadcasted_iota(jnp.int32, (cols, cols), 1)
    unperm = (w == jnp.where(p < half, 2 * p, 2 * p - cols + 1)).astype(F32)
    wpb = wp[...].astype(BF16)

    for t in range(pairs // B):
        i0 = t * B
        acc = None
        for a in range(4):
            for x, w in ((x2, wma), (x3, wmb)):
                part = dot_nt(taps(x, i0, B, a, half), w[:, a * 4 * C : (a + 1) * 4 * C])
                acc = part if acc is None else acc + part
        merged = silu(acc).astype(BF16)
        update = dot_nt(wpb, merged)
        lines = []
        plain = [own_ref[g].astype(F32).T for g in range(groups)]
        for b in range(B):
            u = update[:, b * half : (b + 1) * half]
            for q in range(2):
                line = jnp.concatenate([u[2 * q * COUT : (2 * q + 1) * COUT], u[(2 * q + 1) * COUT : (2 * q + 2) * COUT]], axis=1)
                h = 2 * (i0 + b) + q
                at = (h % PER) * channels
                lines.append(line + plain[h // PER][at : at + COUT])
        woven = jnp.dot(jnp.concatenate(lines, axis=0), unperm, precision=lax.Precision.HIGHEST, preferred_element_type=F32)
        for m in range(2 * B):
            out_ref[:, 2 * i0 + m, :] = woven[m * COUT : (m + 1) * COUT]


def shards(latlon, table, k1, k2, kd, kc, ku, km, kp):
    n = lax.axis_size("lon")
    channels, sub_rows, width = latlon.shape
    height, cols = table.shape[1], table.shape[2]
    lat = jnp.swapaxes(latlon, 0, 1).reshape(sub_rows * channels, width)
    vm = pl.BlockSpec(memory_space=pltpu.VMEM)
    groups = height // PER
    edges = jax.ShapeDtypeStruct((groups, 2 * HALO, PER * channels), BF16)
    corner = jax.ShapeDtypeStruct((2 * HALO, PER * channels), BF16)
    C, C2, COUT = k1.shape[2], kd.shape[2], kp.shape[0]
    weights = (
        jax.ShapeDtypeStruct((2 * C * PER, 4 * PER * channels), BF16),
        jax.ShapeDtypeStruct((2 * C, 4 * PER * channels), BF16),
        jax.ShapeDtypeStruct((2 * C, 4 * PER * channels), BF16),
        jax.ShapeDtypeStruct((2 * C, 4 * PER * channels), BF16),
        jax.ShapeDtypeStruct((4 * C, 16 * C), BF16),
        jax.ShapeDtypeStruct((C2, 12 * C), BF16),
        jax.ShapeDtypeStruct((C2, 9 * C2), BF16),
        jax.ShapeDtypeStruct((4 * C, 4 * C2), BF16),
        jax.ShapeDtypeStruct((4 * C, 16 * C), BF16),
        jax.ShapeDtypeStruct((4 * C, 16 * C), BF16),
        jax.ShapeDtypeStruct((4 * COUT, 4 * C), F32),
    )
    ready = pl.pallas_call(
        functools.partial(exchange_kernel, n),
        out_shape=(jax.ShapeDtypeStruct((groups, cols, PER * channels), BF16), edges, edges,
                   jax.ShapeDtypeStruct((cols, PER * channels), BF16), corner, corner) + weights,
        in_specs=[vm] * 9,
        out_specs=(vm,) * 17,
        scratch_shapes=[
            pltpu.VMEM((n, sub_rows * channels, cols), BF16),
            pltpu.VMEM((2, groups, 2 * HALO, PER * channels), BF16),
            pltpu.SemaphoreType.DMA((n - 1,)),
            pltpu.SemaphoreType.DMA((n - 1,)),
            pltpu.SemaphoreType.DMA,
            pltpu.SemaphoreType.DMA((5,)),
            pltpu.SemaphoreType.DMA((5,)),
        ],
        compiler_params=pltpu.CompilerParams(collective_id=0, has_side_effects=True, vmem_limit_bytes=32 * 2**20),
        name="exchange",
    )(lat, table, k1, k2, kd, kc, ku, km, kp)
    J = cols // 2 + 2 * HALO
    pairs = height // 2
    return pl.pallas_call(
        unet_kernel,
        out_shape=jax.ShapeDtypeStruct((COUT, height, cols), F32),
        in_specs=[vm] * 17,
        out_specs=vm,
        scratch_shapes=[
            pltpu.VMEM((height // PER + 1, J, 4 * PER * channels), BF16),
            pltpu.VMEM((pairs + 5, 2, J, 4 * C), BF16),
            pltpu.VMEM((pairs + 4, 2, J, 4 * C), BF16),
            pltpu.VMEM((pairs + 1, 2, J, 4 * C), BF16),
            pltpu.VMEM((pairs + 5, J, 3 * C2), BF16),
            pltpu.VMEM((pairs + 2, J, 2 * C2), BF16),
        ],
        compiler_params=pltpu.CompilerParams(vmem_limit_bytes=32 * 2**20),
        name="unet",
    )(*ready)


def solution(mesh):
    return jax.shard_map(
        shards,
        mesh=mesh,
        in_specs=(P("groups", "lon", None), P(None, None, "lon")) + (P(),) * 7,
        out_specs=P("groups", None, "lon"),
        check_vma=False,
    )
```

```python
import functools

import jax
import jax.numpy as jnp
from jax import lax
from jax.experimental import pallas as pl
from jax.experimental.pallas import tpu as pltpu
from jax.sharding import PartitionSpec as P

MESH = pl.DeviceIdType.MESH
F32 = jnp.float32
BF16 = jnp.bfloat16
HALO = 8
PER = 8
OFFSETS = (0, 1, 2, -1)
NT = (((1,), (1,)), ((), ()))


def dot_nt(a, b):
    return lax.dot_general(a, b, NT, preferred_element_type=F32)


def silu(x):
    half = 0.5 * x
    return half * jnp.tanh(half) + half


def clear(*arrays):
    for w in arrays:
        w[...] = jnp.zeros_like(w)


def fill(w, kernel, cin, first_in):
    C = kernel.shape[2]
    for q in range(2):
        for p in range(2):
            for a in range(4):
                for l, off in enumerate(OFFSETS):
                    kr, kcol = a - q, off - p + 1
                    if 0 <= kr < 3 and 0 <= kcol < 3:
                        at = (q * 2 + p) * C
                        lane = a * 4 * cin + l * cin
                        w[at : at + C, lane : lane + cin] = kernel[kr, kcol][:, first_in : first_in + cin]


def fine_weights(k1, k2, km, w1, wlast, wfirst, wnext, w2, wma, wmb):
    C, channels = k2.shape[2], k1.shape[2]
    wide = PER * channels
    clear(w1, wlast, wfirst, wnext, w2, wma, wmb)
    for p in range(2):
        for l, off in enumerate(OFFSETS):
            if not 0 <= off - p + 1 < 3:
                continue
            k = [k1[kr, off - p + 1].astype(F32).T.astype(BF16) for kr in range(3)]
            lane = l * wide
            for r in range(PER):
                at = (r * 2 + p) * C
                for kr in range(3):
                    if 0 <= r + kr - 1 < PER:
                        to = lane + (r + kr - 1) * channels
                        w1[at : at + C, to : to + channels] = k[kr]
            end = lane + (PER - 1) * channels
            wlast[p * C : (p + 1) * C, end : end + channels] = k[0]
            wfirst[p * C : (p + 1) * C, lane : lane + channels] = k[0]
            wnext[p * C : (p + 1) * C, lane : lane + channels] = k[2]
    fill(w2, k2, C, 0)
    fill(wma, km, C, 0)
    fill(wmb, km, C, C)


def coarse_weights(kd, kc, ku, kp, wd, wc, wu, wp):
    C, C2 = kd.shape[2], kd.shape[3]
    COUT = kp.shape[0]
    clear(wd, wc, wu, wp)
    for a in range(3):
        for l, kcol in ((0, 1), (1, 2), (3, 0)):
            wd[:, a * 4 * C + l * C : a * 4 * C + (l + 1) * C] = kd[a, kcol].astype(F32).T.astype(BF16)
        for s, kcol in enumerate((1, 2, 0)):
            wc[:, (a * 3 + s) * C2 : (a * 3 + s + 1) * C2] = kc[a, kcol]
    for q, rows in ((0, ((0, 1),)), (1, ((0, 0), (1, 2)))):
        for p, columns in ((0, ((0, 1),)), (1, ((0, 0), (1, 2)))):
            at = (q * 2 + p) * C
            for ri, kr in rows:
                for ci, kcol in columns:
                    lane = (ri * 2 + ci) * C2
                    wu[at : at + C, lane : lane + C2] = ku[kr, kcol]
    for g in range(4):
        wp[g * COUT : (g + 1) * COUT, g * C : (g + 1) * C] = kp[...].astype(F32)


def exchange_kernel(n, lat_ref, tab_ref, k1, k2, kd, kc, ku, km, kp,
                    own_ref, left_ref, right_ref, anti_ref, anti_left_ref, anti_right_ref,
                    w1, wlast, wfirst, wnext, w2, wd, wc, wu, wma, wmb, wp,
                    recv, edge, send_sem, recv_sem, own_sem, hsend, hrecv):
    me = lax.axis_index("lon")
    group = lax.axis_index("groups")
    cols = recv.shape[2]
    height = tab_ref.shape[1]
    per = height // own_ref.shape[0]
    channels = own_ref.shape[2] // per
    barrier = pltpu.get_barrier_semaphore()

    def greet(d, carry):
        pl.semaphore_signal(barrier, inc=1, device_id=(group, lax.rem(me + d, n)), device_id_type=MESH)
        return carry

    lax.fori_loop(1, n, greet, 0)
    mine = pltpu.make_async_copy(lat_ref.at[:, pl.ds(pl.multiple_of(me * cols, cols), cols)], recv.at[me], own_sem)
    mine.start()
    coarse_weights(kd, kc, ku, kp, wd, wc, wu, wp)
    pl.semaphore_wait(barrier, n - 1)

    def block_copy(d, slot):
        target = lax.rem(me + d, n)
        return pltpu.make_async_remote_copy(
            src_ref=lat_ref.at[:, pl.ds(pl.multiple_of(target * cols, cols), cols)],
            dst_ref=recv.at[slot],
            send_sem=send_sem.at[d - 1],
            recv_sem=recv_sem.at[d - 1],
            device_id=(group, target),
            device_id_type=MESH,
        )

    def send(d, carry):
        block_copy(d, me).start()
        return carry

    lax.fori_loop(1, n, send, 0)

    fine_weights(k1, k2, km, w1, wlast, wfirst, wnext, w2, wma, wmb)

    p = lax.broadcasted_iota(jnp.int32, (cols, cols), 0)
    w = lax.broadcasted_iota(jnp.int32, (cols, cols), 1)
    half = cols // 2
    perm = (w == jnp.where(p < half, 2 * p, 2 * p - cols + 1)).astype(F32).astype(BF16)
    rows_at = dot_nt(perm, tab_ref[0].astype(F32).astype(BF16)).astype(jnp.int32)
    cols_at = dot_nt(perm, (tab_ref[1] - me * cols).astype(F32).astype(BF16)).astype(jnp.int32)
    wide = per * channels
    lane = lax.broadcasted_iota(jnp.int32, (cols, wide), 1)
    hots = [(cols_at[:, h : h + 1] == w).astype(F32).astype(BF16) for h in range(height)]
    at_row = [jnp.broadcast_to(rows_at[:, h : h + 1], (cols, wide)) - lane // channels for h in range(height)]
    fi = lax.broadcasted_iota(jnp.int32, (per * wide, wide), 0)
    fo = lax.broadcasted_iota(jnp.int32, (per * wide, wide), 1)
    fold = ((fi // wide == fo // channels) & (fi % channels == fo % channels)).astype(F32).astype(BF16)

    mine.wait()

    def receive(d, carry):
        block_copy(d, lax.rem(me - d + n, n)).wait_recv()
        return carry

    lax.fori_loop(1, n, receive, 0)

    def halo(k, src, dst, shift):
        return pltpu.make_async_remote_copy(
            src_ref=src, dst_ref=dst, send_sem=hsend.at[k], recv_sem=hrecv.at[k],
            device_id=(group, lax.rem(me + shift + 2 * n, n)), device_id_type=MESH)

    copies = [
        halo(0, own_ref.at[0], anti_ref, n // 2),
        halo(1, edge.at[1, 0], anti_left_ref, n // 2 + 1),
        halo(2, edge.at[0, 0], anti_right_ref, n // 2 - 1),
        halo(3, edge.at[1], left_ref, 1),
        halo(4, edge.at[0], right_ref, -1),
    ]
    source = recv[...].reshape(n * lat_ref.shape[0], cols)
    tiles = source.shape[0] // wide
    for g in range(own_ref.shape[0]):
        got = dot_nt(jnp.concatenate(hots[g * per : (g + 1) * per], axis=0), source)
        picked = []
        for q in range(per):
            one = jnp.zeros((cols, wide), F32)
            for t in range(tiles):
                value = got[q * cols : (q + 1) * cols, t * wide : (t + 1) * wide]
                one = jnp.where(at_row[g * per + q] == t * per, value, one)
            picked.append(one.astype(BF16))
        block = jnp.dot(jnp.concatenate(picked, axis=1), fold, preferred_element_type=F32)
        own_ref[g] = block.astype(BF16)
        edge[0, g] = jnp.concatenate([block[0:HALO], block[half : half + HALO]], axis=0).astype(BF16)
        edge[1, g] = jnp.concatenate([block[half - HALO : half], block[cols - HALO : cols]], axis=0).astype(BF16)
        if g == 0:
            for c in copies[:3]:
                c.start()

    for c in copies[3:]:
        c.start()

    def sent(d, carry):
        block_copy(d, me).wait_send()
        return carry

    lax.fori_loop(1, n, sent, 0)
    for c in copies:
        c.wait()


def unet_kernel(own_ref, left_ref, right_ref, anti_ref, anti_left_ref, anti_right_ref,
                w1, wlast, wfirst, wnext, w2, wd, wc, wu, wma, wmb, wp, out_ref, xf, x1, x2, x3, xc, xu):
    groups, cols, wide = own_ref.shape
    height = groups * PER
    channels = wide // PER
    half = cols // 2
    J = half + 2 * HALO
    C = w2.shape[0] // 4
    C2 = wd.shape[0]
    COUT = wp.shape[0] // 4
    pairs = height // 2
    AB = pairs + 1

    def spread(g, l, r):
        even = jnp.concatenate([g[:half], r[:HALO], l[:HALO]], axis=0)
        odd = jnp.concatenate([g[half:], r[HALO:], l[HALO:]], axis=0)
        return jnp.concatenate([even, odd, pltpu.roll(even, J - 1, 0), pltpu.roll(odd, 1, 0)], axis=1).astype(BF16)

    for g in range(groups):
        xf[g] = spread(own_ref[g].astype(F32), left_ref[g].astype(F32), right_ref[g].astype(F32))
    xf[groups] = spread(anti_ref[...].astype(F32), anti_left_ref[...].astype(F32), anti_right_ref[...].astype(F32))

    def neighbours(v):
        count = v.shape[0]
        v = v.reshape(count // J, J, v.shape[1])
        lane = lax.broadcasted_iota(jnp.int32, v.shape, 2)
        other = jnp.where(lane < C, pltpu.roll(v, J - 1, 1), pltpu.roll(v, 1, 1))
        return jnp.concatenate([v, other], axis=2).astype(BF16)

    def store_pair(x, i0, count, s):
        x[pl.ds(i0, count), 1] = neighbours(s[:, : 2 * C])
        x[pl.ds(i0 + 1, count), 0] = neighbours(s[:, 2 * C :])

    def wrap(x):
        x[0, 0] = x[AB, 1]
        x[AB, 0] = x[0, 1]
        x[AB - 1, 1] = jnp.zeros(x.shape[2:], BF16)

    def taps(x, i0, count, a, width):
        v = x[pl.ds(i0 + a // 2, count), a % 2, 0:width]
        return v.reshape(count * width, v.shape[-1])

    B = pairs

    def own_loop(steps, body):
        for t in range(steps):
            body(t)

    every = groups + 1
    acc = dot_nt(xf[...].reshape(every * J, 4 * wide), w1[...]).reshape(every, J, PER * 2 * C)
    from_last = dot_nt(xf[pl.ds(0, groups - 1)].reshape((groups - 1) * J, 4 * wide), wlast[...]).reshape(groups - 1, J, 2 * C)
    from_next = dot_nt(xf[pl.ds(1, groups - 1)].reshape((groups - 1) * J, 4 * wide), wnext[...]).reshape(groups - 1, J, 2 * C)
    own_top = dot_nt(xf[groups], wfirst[...])
    anti_top = dot_nt(xf[0], wfirst[...])
    for g in range(every):
        for r in range(PER):
            v = acc[g, :, r * 2 * C : (r + 1) * 2 * C]
            if r == 0:
                v = v + (anti_top if g == groups else own_top if g == 0 else from_last[g - 1])
            if r == PER - 1 and g < groups - 1:
                v = v + from_next[g]
            slot = g * PER + r + 1 + (2 if g == groups else 0)
            if slot // 2 < x1.shape[0]:
                x1[slot // 2, slot % 2] = neighbours(silu(v))[0]
    wrap(x1)

    def second(i0, count):
        acc = dot_nt(taps(x1, i0, count, 0, J), w2[:, : 4 * C])
        for a in range(1, 4):
            acc += dot_nt(taps(x1, i0, count, a, J), w2[:, a * 4 * C : (a + 1) * 4 * C])
        store_pair(x2, i0, count, silu(acc))

    second(AB, 2)
    own_loop(pairs // B, lambda t: second(t * B, B))
    wrap(x2)

    def shifts(v, both):
        v = v.reshape(v.shape[0] // J, J, v.shape[1])
        parts = [v, pltpu.roll(v, J - 1, 1)]
        if both:
            parts.append(pltpu.roll(v, 1, 1))
        return jnp.concatenate(parts, axis=2).astype(BF16)

    def down(i0, slot, count):
        acc = dot_nt(taps(x2, i0, count, 0, J), wd[:, : 4 * C])
        for a in range(1, 3):
            acc += dot_nt(taps(x2, i0, count, a, J), wd[:, a * 4 * C : (a + 1) * 4 * C])
        xc[pl.ds(slot, count)] = shifts(silu(acc), True)

    down(AB, pairs + 3, 2)
    own_loop(pairs // B, lambda t: down(t * B, t * B + 1, B))
    xc[0] = xc[pairs + 3]
    xc[pairs + 2] = xc[1]
    xc[pairs + 1] = jnp.zeros(xc.shape[1:], BF16)

    def coarse(i0, slot, count):
        acc = None
        for a in range(3):
            v = xc[pl.ds(i0 + a, count)].reshape(count * J, 3 * C2)
            part = dot_nt(v, wc[:, a * 3 * C2 : (a + 1) * 3 * C2])
            acc = part if acc is None else acc + part
        xu[pl.ds(slot, count)] = shifts(silu(acc), False)

    coarse(pairs + 2, pairs + 1, 1)
    own_loop(pairs // B, lambda t: coarse(t * B, t * B, B))
    xu[pairs] = jnp.zeros(xu.shape[1:], BF16)

    def up(i0, count):
        acc = dot_nt(xu[pl.ds(i0, count)].reshape(count * J, 2 * C2), wu[:, : 2 * C2])
        return silu(acc + dot_nt(xu[pl.ds(i0 + 1, count)].reshape(count * J, 2 * C2), wu[:, 2 * C2 :]))

    def up_own(t):
        store_pair(x3, t * B, B, up(t * B, B))

    own_loop(pairs // B, up_own)
    v = xu[pairs + 1]
    x3[0, 0] = neighbours(silu(dot_nt(v, wu[0 : 2 * C, : 2 * C2])))[0]
    x3[AB - 1, 1] = jnp.zeros(x3.shape[2:], BF16)

    p = lax.broadcasted_iota(jnp.int32, (cols, cols), 0)
    w = lax.broadcasted_iota(jnp.int32, (cols, cols), 1)
    unperm = (w == jnp.where(p < half, 2 * p, 2 * p - cols + 1)).astype(F32)
    wpb = wp[...].astype(BF16)

    for t in range(pairs // B):
        i0 = t * B
        acc = None
        for a in range(4):
            for x, w in ((x2, wma), (x3, wmb)):
                part = dot_nt(taps(x, i0, B, a, half), w[:, a * 4 * C : (a + 1) * 4 * C])
                acc = part if acc is None else acc + part
        merged = silu(acc).astype(BF16)
        update = dot_nt(wpb, merged)
        lines = []
        plain = [own_ref[g].astype(F32).T for g in range(groups)]
        for b in range(B):
            u = update[:, b * half : (b + 1) * half]
            for q in range(2):
                line = jnp.concatenate([u[2 * q * COUT : (2 * q + 1) * COUT], u[(2 * q + 1) * COUT : (2 * q + 2) * COUT]], axis=1)
                h = 2 * (i0 + b) + q
                at = (h % PER) * channels
                lines.append(line + plain[h // PER][at : at + COUT])
        woven = jnp.dot(jnp.concatenate(lines, axis=0), unperm, precision=lax.Precision.HIGHEST, preferred_element_type=F32)
        for m in range(2 * B):
            out_ref[:, 2 * i0 + m, :] = woven[m * COUT : (m + 1) * COUT]


def shards(latlon, table, k1, k2, kd, kc, ku, km, kp):
    n = lax.axis_size("lon")
    channels, sub_rows, width = latlon.shape
    height, cols = table.shape[1], table.shape[2]
    lat = jnp.swapaxes(latlon, 0, 1).reshape(sub_rows * channels, width)
    vm = pl.BlockSpec(memory_space=pltpu.VMEM)
    groups = height // PER
    edges = jax.ShapeDtypeStruct((groups, 2 * HALO, PER * channels), BF16)
    corner = jax.ShapeDtypeStruct((2 * HALO, PER * channels), BF16)
    C, C2, COUT = k1.shape[2], kd.shape[2], kp.shape[0]
    weights = (
        jax.ShapeDtypeStruct((2 * C * PER, 4 * PER * channels), BF16),
        jax.ShapeDtypeStruct((2 * C, 4 * PER * channels), BF16),
        jax.ShapeDtypeStruct((2 * C, 4 * PER * channels), BF16),
        jax.ShapeDtypeStruct((2 * C, 4 * PER * channels), BF16),
        jax.ShapeDtypeStruct((4 * C, 16 * C), BF16),
        jax.ShapeDtypeStruct((C2, 12 * C), BF16),
        jax.ShapeDtypeStruct((C2, 9 * C2), BF16),
        jax.ShapeDtypeStruct((4 * C, 4 * C2), BF16),
        jax.ShapeDtypeStruct((4 * C, 16 * C), BF16),
        jax.ShapeDtypeStruct((4 * C, 16 * C), BF16),
        jax.ShapeDtypeStruct((4 * COUT, 4 * C), F32),
    )
    ready = pl.pallas_call(
        functools.partial(exchange_kernel, n),
        out_shape=(jax.ShapeDtypeStruct((groups, cols, PER * channels), BF16), edges, edges,
                   jax.ShapeDtypeStruct((cols, PER * channels), BF16), corner, corner) + weights,
        in_specs=[vm] * 9,
        out_specs=(vm,) * 17,
        scratch_shapes=[
            pltpu.VMEM((n, sub_rows * channels, cols), BF16),
            pltpu.VMEM((2, groups, 2 * HALO, PER * channels), BF16),
            pltpu.SemaphoreType.DMA((n - 1,)),
            pltpu.SemaphoreType.DMA((n - 1,)),
            pltpu.SemaphoreType.DMA,
            pltpu.SemaphoreType.DMA((5,)),
            pltpu.SemaphoreType.DMA((5,)),
        ],
        compiler_params=pltpu.CompilerParams(collective_id=0, has_side_effects=True, vmem_limit_bytes=32 * 2**20),
        name="exchange",
    )(lat, table, jnp.swapaxes(k1, 2, 3), k2, jnp.swapaxes(kd, 2, 3), kc, ku, km, kp)
    J = cols // 2 + 2 * HALO
    pairs = height // 2
    return pl.pallas_call(
        unet_kernel,
        out_shape=jax.ShapeDtypeStruct((COUT, height, cols), F32),
        in_specs=[vm] * 17,
        out_specs=vm,
        scratch_shapes=[
            pltpu.VMEM((height // PER + 1, J, 4 * PER * channels), BF16),
            pltpu.VMEM((pairs + 5, 2, J, 4 * C), BF16),
            pltpu.VMEM((pairs + 4, 2, J, 4 * C), BF16),
            pltpu.VMEM((pairs + 1, 2, J, 4 * C), BF16),
            pltpu.VMEM((pairs + 5, J, 3 * C2), BF16),
            pltpu.VMEM((pairs + 2, J, 2 * C2), BF16),
        ],
        compiler_params=pltpu.CompilerParams(vmem_limit_bytes=32 * 2**20),
        name="unet",
    )(*ready)


def solution(mesh):
    return jax.shard_map(
        shards,
        mesh=mesh,
        in_specs=(P("groups", "lon", None), P(None, None, "lon")) + (P(),) * 7,
        out_specs=P("groups", None, "lon"),
        check_vma=False,
    )
```

```python
import functools

import jax
import jax.numpy as jnp
from jax import lax
from jax.experimental import pallas as pl
from jax.experimental.pallas import tpu as pltpu
from jax.sharding import PartitionSpec as P

MESH = pl.DeviceIdType.MESH
F32 = jnp.float32
BF16 = jnp.bfloat16
HALO = 8
PER = 8
OFFSETS = (0, 1, 2, -1)
NT = (((1,), (1,)), ((), ()))


def dot_nt(a, b):
    return lax.dot_general(a, b, NT, preferred_element_type=F32)


def silu(x):
    half = 0.5 * x
    return half * jnp.tanh(half) + half


def clear(*arrays):
    for w in arrays:
        w[...] = jnp.zeros_like(w)


def fill(w, kernel, cin, first_in):
    C = kernel.shape[2]
    for q in range(2):
        for p in range(2):
            for a in range(4):
                for l, off in enumerate(OFFSETS):
                    kr, kcol = a - q, off - p + 1
                    if 0 <= kr < 3 and 0 <= kcol < 3:
                        at = (q * 2 + p) * C
                        lane = a * 4 * cin + l * cin
                        w[at : at + C, lane : lane + cin] = kernel[kr, kcol][:, first_in : first_in + cin]


def fine_weights(k1, k2, km, w1, wlast, wfirst, wnext, w2, wma, wmb):
    C, channels = k1.shape[2], k1.shape[3]
    wide = PER * channels
    clear(w1, wlast, wfirst, wnext, w2, wma, wmb)
    for p in range(2):
        for l, off in enumerate(OFFSETS):
            if not 0 <= off - p + 1 < 3:
                continue
            k = [k1[kr, off - p + 1] for kr in range(3)]
            lane = l * wide
            for r in range(PER):
                at = (r * 2 + p) * C
                for kr in range(3):
                    if 0 <= r + kr - 1 < PER:
                        to = lane + (r + kr - 1) * channels
                        w1[at : at + C, to : to + channels] = k[kr]
            end = lane + (PER - 1) * channels
            wlast[p * C : (p + 1) * C, end : end + channels] = k[0]
            wfirst[p * C : (p + 1) * C, lane : lane + channels] = k[0]
            wnext[p * C : (p + 1) * C, lane : lane + channels] = k[2]
    fill(w2, k2, C, 0)
    fill(wma, km, C, 0)
    fill(wmb, km, C, C)


def coarse_weights(kd, kc, ku, kp, wd, wc, wu, wp):
    C2, C = kd.shape[2], kd.shape[3]
    COUT = kp.shape[0]
    clear(wd, wc, wu, wp)
    for a in range(3):
        for l, kcol in ((0, 1), (1, 2), (3, 0)):
            wd[:, a * 4 * C + l * C : a * 4 * C + (l + 1) * C] = kd[a, kcol]
        for s, kcol in enumerate((1, 2, 0)):
            wc[:, (a * 3 + s) * C2 : (a * 3 + s + 1) * C2] = kc[a, kcol]
    for q, rows in ((0, ((0, 1),)), (1, ((0, 0), (1, 2)))):
        for p, columns in ((0, ((0, 1),)), (1, ((0, 0), (1, 2)))):
            at = (q * 2 + p) * C
            for ri, kr in rows:
                for ci, kcol in columns:
                    lane = (ri * 2 + ci) * C2
                    wu[at : at + C, lane : lane + C2] = ku[kr, kcol]
    for g in range(4):
        wp[g * COUT : (g + 1) * COUT, g * C : (g + 1) * C] = kp[...].astype(F32)


def exchange_kernel(n, lat_ref, tab_ref, k1, k2, kd, kc, ku, km, kp,
                    own_ref, left_ref, right_ref, anti_ref, anti_left_ref, anti_right_ref,
                    w1, wlast, wfirst, wnext, w2, wd, wc, wu, wma, wmb, wp,
                    recv, edge, send_sem, recv_sem, own_sem, hsend, hrecv):
    me = lax.axis_index("lon")
    group = lax.axis_index("groups")
    cols = recv.shape[2]
    height = tab_ref.shape[1]
    per = height // own_ref.shape[0]
    channels = own_ref.shape[2] // per
    barrier = pltpu.get_barrier_semaphore()

    def greet(d, carry):
        pl.semaphore_signal(barrier, inc=1, device_id=(group, lax.rem(me + d, n)), device_id_type=MESH)
        return carry

    lax.fori_loop(1, n, greet, 0)
    mine = pltpu.make_async_copy(lat_ref.at[:, pl.ds(pl.multiple_of(me * cols, cols), cols)], recv.at[me], own_sem)
    mine.start()
    coarse_weights(kd, kc, ku, kp, wd, wc, wu, wp)
    pl.semaphore_wait(barrier, n - 1)

    def block_copy(d, slot):
        target = lax.rem(me + d, n)
        return pltpu.make_async_remote_copy(
            src_ref=lat_ref.at[:, pl.ds(pl.multiple_of(target * cols, cols), cols)],
            dst_ref=recv.at[slot],
            send_sem=send_sem.at[d - 1],
            recv_sem=recv_sem.at[d - 1],
            device_id=(group, target),
            device_id_type=MESH,
        )

    def send(d, carry):
        block_copy(d, me).start()
        return carry

    lax.fori_loop(1, n, send, 0)

    fine_weights(k1, k2, km, w1, wlast, wfirst, wnext, w2, wma, wmb)

    p = lax.broadcasted_iota(jnp.int32, (cols, cols), 0)
    w = lax.broadcasted_iota(jnp.int32, (cols, cols), 1)
    half = cols // 2
    perm = (w == jnp.where(p < half, 2 * p, 2 * p - cols + 1)).astype(F32).astype(BF16)
    rows_at = dot_nt(perm, tab_ref[0].astype(F32).astype(BF16)).astype(jnp.int32)
    cols_at = dot_nt(perm, (tab_ref[1] - me * cols).astype(F32).astype(BF16)).astype(jnp.int32)
    wide = per * channels
    lane = lax.broadcasted_iota(jnp.int32, (cols, wide), 1)
    hots = [(cols_at[:, h : h + 1] == w).astype(F32).astype(BF16) for h in range(height)]
    at_row = [jnp.broadcast_to(rows_at[:, h : h + 1], (cols, wide)) - lane // channels for h in range(height)]
    fi = lax.broadcasted_iota(jnp.int32, (per * wide, wide), 0)
    fo = lax.broadcasted_iota(jnp.int32, (per * wide, wide), 1)
    fold = ((fi // wide == fo // channels) & (fi % channels == fo % channels)).astype(F32).astype(BF16)

    mine.wait()

    def receive(d, carry):
        block_copy(d, lax.rem(me - d + n, n)).wait_recv()
        return carry

    lax.fori_loop(1, n, receive, 0)

    def halo(k, src, dst, shift):
        return pltpu.make_async_remote_copy(
            src_ref=src, dst_ref=dst, send_sem=hsend.at[k], recv_sem=hrecv.at[k],
            device_id=(group, lax.rem(me + shift + 2 * n, n)), device_id_type=MESH)

    copies = [
        halo(0, own_ref.at[0], anti_ref, n // 2),
        halo(1, edge.at[1, 0], anti_left_ref, n // 2 + 1),
        halo(2, edge.at[0, 0], anti_right_ref, n // 2 - 1),
        halo(3, edge.at[1], left_ref, 1),
        halo(4, edge.at[0], right_ref, -1),
    ]
    source = recv[...].reshape(n * lat_ref.shape[0], cols)
    tiles = source.shape[0] // wide
    for g in range(own_ref.shape[0]):
        got = dot_nt(jnp.concatenate(hots[g * per : (g + 1) * per], axis=0), source)
        picked = []
        for q in range(per):
            one = jnp.zeros((cols, wide), F32)
            for t in range(tiles):
                value = got[q * cols : (q + 1) * cols, t * wide : (t + 1) * wide]
                one = jnp.where(at_row[g * per + q] == t * per, value, one)
            picked.append(one.astype(BF16))
        block = jnp.dot(jnp.concatenate(picked, axis=1), fold, preferred_element_type=F32)
        own_ref[g] = block.astype(BF16)
        edge[0, g] = jnp.concatenate([block[0:HALO], block[half : half + HALO]], axis=0).astype(BF16)
        edge[1, g] = jnp.concatenate([block[half - HALO : half], block[cols - HALO : cols]], axis=0).astype(BF16)
        if g == 0:
            for c in copies[:3]:
                c.start()

    for c in copies[3:]:
        c.start()

    def sent(d, carry):
        block_copy(d, me).wait_send()
        return carry

    lax.fori_loop(1, n, sent, 0)
    for c in copies:
        c.wait()


def unet_kernel(own_ref, left_ref, right_ref, anti_ref, anti_left_ref, anti_right_ref,
                w1, wlast, wfirst, wnext, w2, wd, wc, wu, wma, wmb, wp, out_ref, xf, x1, x2, x3, xc, xu):
    groups, cols, wide = own_ref.shape
    height = groups * PER
    channels = wide // PER
    half = cols // 2
    J = half + 2 * HALO
    C = w2.shape[0] // 4
    C2 = wd.shape[0]
    COUT = wp.shape[0] // 4
    pairs = height // 2
    AB = pairs + 1

    def spread(g, l, r):
        even = jnp.concatenate([g[:half], r[:HALO], l[:HALO]], axis=0)
        odd = jnp.concatenate([g[half:], r[HALO:], l[HALO:]], axis=0)
        return jnp.concatenate([even, odd, pltpu.roll(even, J - 1, 0), pltpu.roll(odd, 1, 0)], axis=1).astype(BF16)

    for g in range(groups):
        xf[g] = spread(own_ref[g].astype(F32), left_ref[g].astype(F32), right_ref[g].astype(F32))
    xf[groups] = spread(anti_ref[...].astype(F32), anti_left_ref[...].astype(F32), anti_right_ref[...].astype(F32))

    def neighbours(v):
        count = v.shape[0]
        v = v.reshape(count // J, J, v.shape[1])
        lane = lax.broadcasted_iota(jnp.int32, v.shape, 2)
        other = jnp.where(lane < C, pltpu.roll(v, J - 1, 1), pltpu.roll(v, 1, 1))
        return jnp.concatenate([v, other], axis=2).astype(BF16)

    def store_pair(x, i0, count, s):
        x[pl.ds(i0, count), 1] = neighbours(s[:, : 2 * C])
        x[pl.ds(i0 + 1, count), 0] = neighbours(s[:, 2 * C :])

    def wrap(x):
        x[0, 0] = x[AB, 1]
        x[AB, 0] = x[0, 1]
        x[AB - 1, 1] = jnp.zeros(x.shape[2:], BF16)

    def taps(x, i0, count, a, width):
        v = x[pl.ds(i0 + a // 2, count), a % 2, 0:width]
        return v.reshape(count * width, v.shape[-1])

    B = pairs

    def own_loop(steps, body):
        for t in range(steps):
            body(t)

    every = groups + 1
    acc = dot_nt(xf[...].reshape(every * J, 4 * wide), w1[...]).reshape(every, J, PER * 2 * C)
    from_last = dot_nt(xf[pl.ds(0, groups - 1)].reshape((groups - 1) * J, 4 * wide), wlast[...]).reshape(groups - 1, J, 2 * C)
    from_next = dot_nt(xf[pl.ds(1, groups - 1)].reshape((groups - 1) * J, 4 * wide), wnext[...]).reshape(groups - 1, J, 2 * C)
    own_top = dot_nt(xf[groups], wfirst[...])
    anti_top = dot_nt(xf[0], wfirst[...])
    for g in range(every):
        for r in range(PER):
            v = acc[g, :, r * 2 * C : (r + 1) * 2 * C]
            if r == 0:
                v = v + (anti_top if g == groups else own_top if g == 0 else from_last[g - 1])
            if r == PER - 1 and g < groups - 1:
                v = v + from_next[g]
            slot = g * PER + r + 1 + (2 if g == groups else 0)
            if slot // 2 < x1.shape[0]:
                x1[slot // 2, slot % 2] = neighbours(silu(v))[0]
    wrap(x1)

    def second(i0, count):
        acc = dot_nt(taps(x1, i0, count, 0, J), w2[:, : 4 * C])
        for a in range(1, 4):
            acc += dot_nt(taps(x1, i0, count, a, J), w2[:, a * 4 * C : (a + 1) * 4 * C])
        store_pair(x2, i0, count, silu(acc))

    second(AB, 2)
    own_loop(pairs // B, lambda t: second(t * B, B))
    wrap(x2)

    def shifts(v, both):
        v = v.reshape(v.shape[0] // J, J, v.shape[1])
        parts = [v, pltpu.roll(v, J - 1, 1)]
        if both:
            parts.append(pltpu.roll(v, 1, 1))
        return jnp.concatenate(parts, axis=2).astype(BF16)

    def down(i0, slot, count):
        acc = dot_nt(taps(x2, i0, count, 0, J), wd[:, : 4 * C])
        for a in range(1, 3):
            acc += dot_nt(taps(x2, i0, count, a, J), wd[:, a * 4 * C : (a + 1) * 4 * C])
        xc[pl.ds(slot, count)] = shifts(silu(acc), True)

    down(AB, pairs + 3, 2)
    own_loop(pairs // B, lambda t: down(t * B, t * B + 1, B))
    xc[0] = xc[pairs + 3]
    xc[pairs + 2] = xc[1]
    xc[pairs + 1] = jnp.zeros(xc.shape[1:], BF16)

    def coarse(i0, slot, count):
        acc = None
        for a in range(3):
            v = xc[pl.ds(i0 + a, count)].reshape(count * J, 3 * C2)
            part = dot_nt(v, wc[:, a * 3 * C2 : (a + 1) * 3 * C2])
            acc = part if acc is None else acc + part
        xu[pl.ds(slot, count)] = shifts(silu(acc), False)

    coarse(pairs + 2, pairs + 1, 1)
    own_loop(pairs // B, lambda t: coarse(t * B, t * B, B))
    xu[pairs] = jnp.zeros(xu.shape[1:], BF16)

    def up(i0, count):
        acc = dot_nt(xu[pl.ds(i0, count)].reshape(count * J, 2 * C2), wu[:, : 2 * C2])
        return silu(acc + dot_nt(xu[pl.ds(i0 + 1, count)].reshape(count * J, 2 * C2), wu[:, 2 * C2 :]))

    def up_own(t):
        store_pair(x3, t * B, B, up(t * B, B))

    own_loop(pairs // B, up_own)
    v = xu[pairs + 1]
    x3[0, 0] = neighbours(silu(dot_nt(v, wu[0 : 2 * C, : 2 * C2])))[0]
    x3[AB - 1, 1] = jnp.zeros(x3.shape[2:], BF16)

    p = lax.broadcasted_iota(jnp.int32, (cols, cols), 0)
    w = lax.broadcasted_iota(jnp.int32, (cols, cols), 1)
    unperm = (w == jnp.where(p < half, 2 * p, 2 * p - cols + 1)).astype(F32)
    wpb = wp[...].astype(BF16)

    for t in range(pairs // B):
        i0 = t * B
        acc = None
        for a in range(4):
            for x, w in ((x2, wma), (x3, wmb)):
                part = dot_nt(taps(x, i0, B, a, half), w[:, a * 4 * C : (a + 1) * 4 * C])
                acc = part if acc is None else acc + part
        merged = silu(acc).astype(BF16)
        update = dot_nt(wpb, merged)
        lines = []
        plain = [own_ref[g].astype(F32).T for g in range(groups)]
        for b in range(B):
            u = update[:, b * half : (b + 1) * half]
            for q in range(2):
                line = jnp.concatenate([u[2 * q * COUT : (2 * q + 1) * COUT], u[(2 * q + 1) * COUT : (2 * q + 2) * COUT]], axis=1)
                h = 2 * (i0 + b) + q
                at = (h % PER) * channels
                lines.append(line + plain[h // PER][at : at + COUT])
        woven = jnp.dot(jnp.concatenate(lines, axis=0), unperm, precision=lax.Precision.HIGHEST, preferred_element_type=F32)
        for m in range(2 * B):
            out_ref[:, 2 * i0 + m, :] = woven[m * COUT : (m + 1) * COUT]


def shards(latlon, table, k1, k2, kd, kc, ku, km, kp):
    n = lax.axis_size("lon")
    channels, sub_rows, width = latlon.shape
    height, cols = table.shape[1], table.shape[2]
    lat = jnp.swapaxes(latlon, 0, 1).reshape(sub_rows * channels, width)
    vm = pl.BlockSpec(memory_space=pltpu.VMEM)
    groups = height // PER
    edges = jax.ShapeDtypeStruct((groups, 2 * HALO, PER * channels), BF16)
    corner = jax.ShapeDtypeStruct((2 * HALO, PER * channels), BF16)
    C, C2, COUT = k1.shape[2], kd.shape[2], kp.shape[0]
    weights = (
        jax.ShapeDtypeStruct((2 * C * PER, 4 * PER * channels), BF16),
        jax.ShapeDtypeStruct((2 * C, 4 * PER * channels), BF16),
        jax.ShapeDtypeStruct((2 * C, 4 * PER * channels), BF16),
        jax.ShapeDtypeStruct((2 * C, 4 * PER * channels), BF16),
        jax.ShapeDtypeStruct((4 * C, 16 * C), BF16),
        jax.ShapeDtypeStruct((C2, 12 * C), BF16),
        jax.ShapeDtypeStruct((C2, 9 * C2), BF16),
        jax.ShapeDtypeStruct((4 * C, 4 * C2), BF16),
        jax.ShapeDtypeStruct((4 * C, 16 * C), BF16),
        jax.ShapeDtypeStruct((4 * C, 16 * C), BF16),
        jax.ShapeDtypeStruct((4 * COUT, 4 * C), F32),
    )
    ready = pl.pallas_call(
        functools.partial(exchange_kernel, n),
        out_shape=(jax.ShapeDtypeStruct((groups, cols, PER * channels), BF16), edges, edges,
                   jax.ShapeDtypeStruct((cols, PER * channels), BF16), corner, corner) + weights,
        in_specs=[vm] * 9,
        out_specs=(vm,) * 17,
        scratch_shapes=[
            pltpu.VMEM((n, sub_rows * channels, cols), BF16),
            pltpu.VMEM((2, groups, 2 * HALO, PER * channels), BF16),
            pltpu.SemaphoreType.DMA((n - 1,)),
            pltpu.SemaphoreType.DMA((n - 1,)),
            pltpu.SemaphoreType.DMA,
            pltpu.SemaphoreType.DMA((5,)),
            pltpu.SemaphoreType.DMA((5,)),
        ],
        compiler_params=pltpu.CompilerParams(collective_id=0, has_side_effects=True, vmem_limit_bytes=32 * 2**20),
        name="exchange",
    )(lat, table, k1, k2, kd, kc, ku, km, kp)
    J = cols // 2 + 2 * HALO
    pairs = height // 2
    return pl.pallas_call(
        unet_kernel,
        out_shape=jax.ShapeDtypeStruct((COUT, height, cols), F32),
        in_specs=[vm] * 17,
        out_specs=vm,
        scratch_shapes=[
            pltpu.VMEM((height // PER + 1, J, 4 * PER * channels), BF16),
            pltpu.VMEM((pairs + 5, 2, J, 4 * C), BF16),
            pltpu.VMEM((pairs + 4, 2, J, 4 * C), BF16),
            pltpu.VMEM((pairs + 1, 2, J, 4 * C), BF16),
            pltpu.VMEM((pairs + 5, J, 3 * C2), BF16),
            pltpu.VMEM((pairs + 2, J, 2 * C2), BF16),
        ],
        compiler_params=pltpu.CompilerParams(vmem_limit_bytes=32 * 2**20),
        name="unet",
    )(*ready)


def solution(mesh):
    return jax.shard_map(
        shards,
        mesh=mesh,
        in_specs=(P("groups", "lon", None), P(None, None, "lon")) + (P(),) * 7,
        out_specs=P("groups", None, "lon"),
        check_vma=False,
    )
```
